32 devices in a mesh: blk: 8 (over z, y), feat: 4 (over x, core).
Axes of the slice: x: 2, y: 2, z: 4, core: 2. Of those that a mesh axis runs over, the one named last changes fastest.
Arguments:
- image: bfloat16 [1408, 1152], P('blk', 'feat'), may hold values from -6 to 6
- text: bfloat16 [1408, 1152], P('blk', 'feat'), may hold values from -6 to 6
- scale: float32 [], replicated, may hold values from 0.05 to 0.12
- bias: float32 [], replicated, may hold values from -7 to -4
Outputs:
- image_grad: float32 [1408, 1152], P('blk', 'feat')
- text_grad: float32 [1408, 1152], P('blk', 'feat')
The draws below stay inside these ranges and needn't reach their ends.
All inputs are finite; a program needn't handle non-finite values.
Results may differ from the reference program's by a relative error of at most 0.0013.
Values may be sent and summed in bfloat16 or wider, within the bound.
A program may use at most 64 MiB of HBM per device.

```python
import math
import jax
import jax.numpy as jnp
from jax import lax

D = 1152
B_DEV = 176
BATCH = 1408
N_BLK = 8


def steps_of(own_key, shape, cuts, low, high):
    level, own = 1.0, jax.random.fold_in(own_key, 6)
    for position, parts in cuts:
        heights = jnp.exp(jax.random.uniform(jax.random.fold_in(own, position), (parts,), jnp.float32, low / len(cuts), high / len(cuts)))
        level = level * jnp.repeat(heights, shape[position] // parts).reshape([-1 if axis == position else 1 for axis in range(len(shape))])
    return level


def centred(rng, extent, deviation, limit, pieces=(), held_as=jnp.bfloat16):
    values = jax.random.normal(rng, extent, jnp.float32) * deviation
    if len(pieces) > 0:
        values = steps_of(rng, extent, pieces, -0.22, 0.18) * values
    return jnp.clip(values, min=-limit, max=limit).astype(held_as)


def setup_inputs(seed: int = 0) -> dict:
    seeds = jax.random.split(jax.random.key(seed), 5)
    image = centred(seeds[0], (BATCH, D), 1.0, 6.0, ((0, 8), (1, 4)))
    text = centred(seeds[1], (BATCH, D), 1.0, 6.0, ((0, 8), (1, 4)))
    scale = jnp.clip(jnp.exp(jax.random.uniform(seeds[2], (), jnp.float32, math.log(0.05), math.log(0.12))), 0.05, 0.12)
    bias = jnp.clip(jax.random.uniform(seeds[3], (), jnp.float32, -7.0, -4.0), -7.0, -4.0)
    return {"image": image, "text": text, "scale": scale, "bias": bias}


def reference(image, text, scale, bias):
    total = image.shape[0]
    blocks = image.reshape(N_BLK, B_DEV, D)
    col_index = jnp.arange(total, dtype=jnp.int32)[None, :]

    def visit(carry, item):
        block_id, rows_img = item
        dots = jnp.dot(rows_img, text.T, preferred_element_type=jnp.float32)
        logit = scale * dots + bias
        row_index = block_id * B_DEV + jnp.arange(B_DEV, dtype=jnp.int32)[:, None]
        slope = jnp.where(row_index == col_index, -jax.nn.sigmoid(-logit), jax.nn.sigmoid(logit)).astype(jnp.bfloat16)
        grad_rows = scale * jnp.dot(slope, text, preferred_element_type=jnp.float32)
        carry = carry + scale * jnp.dot(slope.T, rows_img, preferred_element_type=jnp.float32)
        return carry, grad_rows

    start = jnp.zeros((total, D), jnp.float32)
    text_grad, image_parts = lax.scan(visit, start, (jnp.arange(N_BLK, dtype=jnp.int32), blocks))
    return image_parts.reshape(total, D), text_grad
```

```python
import functools
import jax
import jax.numpy as jnp
from jax import lax
from jax.experimental import pallas as pl
from jax.experimental.pallas import tpu as pltpu
from jax.sharding import PartitionSpec as P


def from_behind(block, axis, distance):
    devices = range(lax.axis_size(axis))
    route = [((i - distance) % len(devices), i) for i in devices]
    return lax.ppermute(block, axis, route)


def pair_grads(image_all, current, scale, bias, diag_start, own):
    dots = lax.dot_general(
        image_all, current, (((1,), (1,)), ((), ())), preferred_element_type=jnp.float32
    )
    logit = scale * dots + bias
    if own:
        row_index = lax.broadcasted_iota(jnp.int32, logit.shape, 0)
        col_index = diag_start + lax.broadcasted_iota(jnp.int32, logit.shape, 1)
        value = jnp.where(row_index == col_index, -jax.nn.sigmoid(-logit), jax.nn.sigmoid(logit))
    else:
        value = jax.nn.sigmoid(logit)
    slope = value.astype(jnp.bfloat16)
    image_add = jnp.dot(slope, current, preferred_element_type=jnp.float32)
    text_add = lax.dot_general(
        slope, image_all, (((0,), (0,)), ((), ())), preferred_element_type=jnp.float32
    )
    return (image_add, text_add)


def pass_both(current, accum):
    return (
        from_behind(current.astype(jnp.float32), "blk", 1).astype(current.dtype),
        from_behind(accum, "blk", 1),
    )


def shards(image, text, scale, bias):
    block_count = lax.axis_size("blk")
    image_all = lax.all_gather(image, "feat", axis=1, tiled=True)
    quarter = lax.all_to_all(text, "feat", split_axis=0, concat_axis=1, tiled=True)
    rows_q = quarter.shape[0]
    diag_start = lax.axis_index("feat") * rows_q
    image_acc, text_acc = pair_grads(image_all, quarter, scale, bias, diag_start, True)

    def visit(step, carry):
        current, accum, grad_img = carry
        current, accum = pass_both(current, accum)
        image_add, text_add = pair_grads(image_all, current, scale, bias, 0, False)
        return (current, accum + text_add, grad_img + image_add)

    current, text_acc, image_acc = lax.fori_loop(
        1, block_count, visit, (quarter, text_acc, image_acc)
    )
    text_acc = from_behind(text_acc, "blk", 1)
    image_grad = scale * lax.psum_scatter(image_acc, "feat", scatter_dimension=1, tiled=True)
    text_grad = lax.all_to_all(scale * text_acc, "feat", split_axis=1, concat_axis=0, tiled=True)
    return (image_grad, text_grad)


MESH = pl.DeviceIdType.MESH
BF16 = jnp.bfloat16
F32 = jnp.float32
GROUP = 32


def round_up(value, unit):
    return -(-value // unit) * unit


def dot_nt(a, b):
    return lax.dot_general(a, b, (((1,), (1,)), ((), ())), preferred_element_type=F32)


def kernel(nz, rows, wide, rem, img_ref, txt_ref, sc_ref, gi_ref, gt_ref,
           buf, rbuf, acc, accr, ssem, rsem):
    blk, feat = lax.axis_index("blk"), lax.axis_index("feat")
    z, y = blk // 2, blk % 2
    x, c = feat // 2, feat % 2
    blk_y = z * 2 + 1 - y
    feat_x = (1 - x) * 2 + c
    feat_c = x * 2 + 1 - c
    feat_xc = (1 - x) * 2 + 1 - c
    near = jnp.minimum(z, nz - 1 - z)
    has_up, has_down = z < nz - 1, z > 0

    barrier = pltpu.get_barrier_semaphore()

    def greet(b, f):
        pl.semaphore_signal(barrier, inc=1, device_id=(b, f), device_id_type=MESH)

    greet(blk_y, feat)
    greet(blk, feat_x)
    greet(blk, feat_c)

    @pl.when(has_up)
    def _():
        greet(blk + 2, feat)

    @pl.when(has_down)
    def _():
        greet(blk - 2, feat)

    for t, ref in ((0, img_ref), (1, txt_ref)):
        buf[t, blk, feat, 0:rows, :] = ref[:, 0:wide]
        last = ref[:, wide:wide + rem]
        for q in range(-(-rows // GROUP)):
            n = min(GROUP, rows - q * GROUP)
            buf[t, blk, feat, rows:rows + n, q * rem:(q + 1) * rem] = last[q * GROUP:q * GROUP + n]

    pl.semaphore_wait(barrier, 3 + jnp.where(has_up, 1, 0) + jnp.where(has_down, 1, 0))

    sent = []

    def copy(t, b, f, to, sid):
        return pltpu.make_async_remote_copy(
            src_ref=buf.at[t, b, f], dst_ref=buf.at[t, b, f],
            send_sem=ssem.at[sid], recv_sem=rsem.at[t, b, f],
            device_id=to, device_id_type=MESH,
        )

    def send(t, b, f, to, cond=None):
        sid = len(sent)
        sent.append((t, b, f, to, cond))
        if cond is None:
            copy(t, b, f, to, sid).start()
        else:
            @pl.when(cond)
            def _():
                copy(t, b, f, to, sid).start()

    def arrive(t, b, f):
        copy(t, b, f, (blk, feat_c), 0).wait_recv()

    def item(i):
        k = jnp.where(i <= 2 * near, (i + 1) // 2, i - near)
        below = jnp.where(i <= 2 * near, i % 2, jnp.where(z > near, 1, 0))
        return jnp.where(below == 1, z - k, z + k), below

    def stage1(i):
        if i == 0:
            zi = z
            for t in (0, 1):
                send(t, blk, feat, (blk + 2, feat), has_up)
                send(t, blk, feat, (blk - 2, feat), has_down)
        else:
            zi, below = item(i)
            onward_up = jnp.logical_and(below == 1, has_up)
            onward_down = jnp.logical_and(below == 0, has_down)
            for t in (0, 1):
                b = zi * 2 + y
                arrive(t, b, feat)
                send(t, b, feat, (blk + 2, feat), onward_up)
                send(t, b, feat, (blk - 2, feat), onward_down)
        b = zi * 2 + y
        for t in (0, 1):
            send(t, b, feat, (blk, feat_x))
            send(t, b, feat, (blk_y, feat))
        for t in (0, 1):
            send(t, b, feat, (blk, feat_c))

    def place(i):
        zi = item(i)[0] if i else z
        return zi * 2 + y, zi * 2 + 1 - y

    def stage2(i):
        own, other = place(i)
        arrive(0, other, feat)
        send(0, other, feat, (blk, feat_x))
        send(0, other, feat, (blk, feat_c))
        arrive(1, own, feat_x)
        send(1, own, feat_x, (blk_y, feat))
        send(1, own, feat_x, (blk, feat_c))

    def stage3(i):
        own, other = place(i)
        for t, b, f in ((0, own, feat_x), (1, other, feat), (0, other, feat_x), (1, other, feat_x)):
            arrive(t, b, f)
            send(t, b, f, (blk, feat_c))

    scale, bias = sc_ref[0], sc_ref[1]

    def unpack(b):
        for t in (0, 1):
            for q in range(-(-rows // GROUP)):
                n = min(GROUP, rows - q * GROUP)
                for f in range(4):
                    rbuf[t, b, q * GROUP:q * GROUP + n, f * rem:(f + 1) * rem] = (
                        buf[t, b, f, rows:rows + n, q * rem:(q + 1) * rem])

    def work(b):
        for t, u in ((0, 1), (1, 0)):
            dots = dot_nt(rbuf[t, blk], rbuf[u, b])
            for f in range(4):
                dots += dot_nt(buf[t, blk, f, 0:rows, :], buf[u, b, f, 0:rows, :])
            logit = scale * dots + bias
            r = lax.broadcasted_iota(jnp.int32, logit.shape, 0)
            col = lax.broadcasted_iota(jnp.int32, logit.shape, 1) + (b - blk) * rows
            diag = r == col
            value = jax.nn.sigmoid(jnp.where(diag, -logit, logit))
            slope = jnp.where(diag, -value, value).astype(BF16)
            acc[t] += jnp.dot(slope, buf[u, b, feat, 0:rows, :], preferred_element_type=F32)
            accr[t] += jnp.dot(slope, rbuf[u, b], preferred_element_type=F32)

    def stage4(i):
        own, other = place(i)
        for t in (0, 1):
            for b in (own, other):
                for f in (feat_c, feat_xc):
                    arrive(t, b, f)
        if i == 0:
            acc[...] = jnp.zeros_like(acc)
            accr[...] = jnp.zeros_like(accr)
        unpack(own)
        unpack(other)

        @pl.loop(0, 2)
        def _(s):
            work(own - y + s)

    for r in range(nz + 3):
        for lag, stage in enumerate((stage1, stage2, stage3, stage4)):
            if 0 <= r - lag < nz:
                stage(r - lag)

    for t, ref in ((0, gi_ref), (1, gt_ref)):
        ref[:, 0:wide] = scale * acc[t]
        for f in range(4):
            @pl.when(feat == f)
            def _():
                ref[:, wide:wide + rem] = scale * accr[t, :, f * rem:(f + 1) * rem]

    for sid, (t, b, f, to, cond) in enumerate(sent):
        if cond is None:
            copy(t, b, f, to, sid).wait_send()
        else:
            @pl.when(cond)
            def _():
                copy(t, b, f, to, sid).wait_send()


def gathered(blocks, image, text, scale, bias):
    rows, width = image.shape
    wide = width // 128 * 128
    rem = width - wide
    nz = blocks // 2
    out = jax.ShapeDtypeStruct((rows, width), F32)
    return pl.pallas_call(
        functools.partial(kernel, nz, rows, wide, rem),
        out_shape=(out, out),
        in_specs=[pl.BlockSpec(memory_space=pltpu.VMEM)] * 2
        + [pl.BlockSpec(memory_space=pltpu.SMEM)],
        out_specs=(pl.BlockSpec(memory_space=pltpu.VMEM),) * 2,
        scratch_shapes=[
            pltpu.VMEM((2, blocks, 4, rows + GROUP, wide), BF16),
            pltpu.VMEM((2, blocks, rows, 4 * rem), BF16),
            pltpu.VMEM((2, rows, wide), F32),
            pltpu.VMEM((2, rows, 4 * rem), F32),
            pltpu.SemaphoreType.DMA((26 * nz,)),
            pltpu.SemaphoreType.DMA((2, blocks, 4)),
        ],
        compiler_params=pltpu.CompilerParams(
            collective_id=0, has_side_effects=True, vmem_limit_bytes=48 * 2**20
        ),
    )(image, text, jnp.stack([scale, bias]))


def solution(mesh):
    in_specs = (P("blk", "feat"), P("blk", "feat"), P(), P())
    out_specs = (P("blk", "feat"), P("blk", "feat"))
    blocks, feats = mesh.shape["blk"], mesh.shape["feat"]

    def body(image, text, scale, bias):
        whole = 2 * blocks * feats * image.size * 2
        if feats == 4 and blocks % 2 == 0 and whole <= 16 * 2**20:
            return gathered(blocks, image, text, scale, bias)
        return shards(image, text, scale, bias)

    return jax.shard_map(body, mesh=mesh, in_specs=in_specs, out_specs=out_specs, check_vma=False)
```

```python
import functools
import jax
import jax.numpy as jnp
from jax import lax
from jax.experimental import pallas as pl
from jax.experimental.pallas import tpu as pltpu
from jax.sharding import PartitionSpec as P


def from_behind(block, axis, distance):
    devices = range(lax.axis_size(axis))
    route = [((i - distance) % len(devices), i) for i in devices]
    return lax.ppermute(block, axis, route)


def pair_grads(image_all, current, scale, bias, diag_start, own):
    dots = lax.dot_general(
        image_all, current, (((1,), (1,)), ((), ())), preferred_element_type=jnp.float32
    )
    logit = scale * dots + bias
    if own:
        row_index = lax.broadcasted_iota(jnp.int32, logit.shape, 0)
        col_index = diag_start + lax.broadcasted_iota(jnp.int32, logit.shape, 1)
        value = jnp.where(row_index == col_index, -jax.nn.sigmoid(-logit), jax.nn.sigmoid(logit))
    else:
        value = jax.nn.sigmoid(logit)
    slope = value.astype(jnp.bfloat16)
    image_add = jnp.dot(slope, current, preferred_element_type=jnp.float32)
    text_add = lax.dot_general(
        slope, image_all, (((0,), (0,)), ((), ())), preferred_element_type=jnp.float32
    )
    return (image_add, text_add)


def pass_both(current, accum):
    return (
        from_behind(current.astype(jnp.float32), "blk", 1).astype(current.dtype),
        from_behind(accum, "blk", 1),
    )


def shards(image, text, scale, bias):
    block_count = lax.axis_size("blk")
    image_all = lax.all_gather(image, "feat", axis=1, tiled=True)
    quarter = lax.all_to_all(text, "feat", split_axis=0, concat_axis=1, tiled=True)
    rows_q = quarter.shape[0]
    diag_start = lax.axis_index("feat") * rows_q
    image_acc, text_acc = pair_grads(image_all, quarter, scale, bias, diag_start, True)

    def visit(step, carry):
        current, accum, grad_img = carry
        current, accum = pass_both(current, accum)
        image_add, text_add = pair_grads(image_all, current, scale, bias, 0, False)
        return (current, accum + text_add, grad_img + image_add)

    current, text_acc, image_acc = lax.fori_loop(
        1, block_count, visit, (quarter, text_acc, image_acc)
    )
    text_acc = from_behind(text_acc, "blk", 1)
    image_grad = scale * lax.psum_scatter(image_acc, "feat", scatter_dimension=1, tiled=True)
    text_grad = lax.all_to_all(scale * text_acc, "feat", split_axis=1, concat_axis=0, tiled=True)
    return (image_grad, text_grad)


MESH = pl.DeviceIdType.MESH
BF16 = jnp.bfloat16
F32 = jnp.float32
GROUP = 32


def round_up(value, unit):
    return -(-value // unit) * unit


def dot_nt(a, b):
    return lax.dot_general(a, b, (((1,), (1,)), ((), ())), preferred_element_type=F32)


def kernel(nz, rows, wide, rem, img_ref, txt_ref, scale_ref, bias_ref, gi_ref, gt_ref,
           own_in, in_sem, buf, rbuf, acc, accr, ssem, rsem):
    blk, feat = lax.axis_index("blk"), lax.axis_index("feat")
    z, y = blk // 2, blk % 2
    x, c = feat // 2, feat % 2
    blk_y = z * 2 + 1 - y
    feat_x = (1 - x) * 2 + c
    feat_c = x * 2 + 1 - c
    feat_xc = (1 - x) * 2 + 1 - c
    cut = (rows + GROUP) * 2 // 5 // 16 * 16
    parts = (
        (0, 0, cut, "zyx"),
        (1, 0, cut, "zxy"),
        (0, cut, rows + GROUP - cut, "yzx"),
        (1, cut, rows + GROUP - cut, "xzy"),
    )
    loads = [pltpu.make_async_copy(ref, own_in.at[t], in_sem.at[t])
             for t, ref in enumerate((img_ref, txt_ref))]
    for load in loads:
        load.start()
    near = jnp.minimum(z, nz - 1 - z)
    has_up, has_down = z < nz - 1, z > 0

    barrier = pltpu.get_barrier_semaphore()

    def greet(b, f):
        pl.semaphore_signal(barrier, inc=1, device_id=(b, f), device_id_type=MESH)

    greet(blk_y, feat)
    greet(blk, feat_x)
    greet(blk, feat_c)

    @pl.when(has_up)
    def _():
        greet(blk + 2, feat)

    @pl.when(has_down)
    def _():
        greet(blk - 2, feat)

    for t in (0, 1):
        loads[t].wait()
        buf[t, blk, feat, 0:rows, :] = own_in[t, :, 0:wide]
        last = own_in[t, :, wide:wide + rem]
        for q in range(-(-rows // GROUP)):
            n = min(GROUP, rows - q * GROUP)
            buf[t, blk, feat, rows:rows + n, q * rem:(q + 1) * rem] = last[q * GROUP:q * GROUP + n]

    pl.semaphore_wait(barrier, 3 + jnp.where(has_up, 1, 0) + jnp.where(has_down, 1, 0))

    sent = []

    def copy(p, b, f, to, sid):
        t, first, n, _ = parts[p]
        slot = buf.at[t, b, f, pl.ds(first, n)]
        return pltpu.make_async_remote_copy(
            src_ref=slot, dst_ref=slot, send_sem=ssem.at[sid], recv_sem=rsem.at[p, b, f],
            device_id=to, device_id_type=MESH,
        )

    def send(p, b, f, to, cond=None):
        sid = len(sent)
        sent.append((p, b, f, to, cond))
        if cond is None:
            copy(p, b, f, to, sid).start()
        else:
            @pl.when(cond)
            def _():
                copy(p, b, f, to, sid).start()

    def arrive(p, b, f):
        copy(p, b, f, (blk, feat_c), 0).wait_recv()

    def item(i):
        k = jnp.where(i <= 2 * near, (i + 1) // 2, i - near)
        below = jnp.where(i <= 2 * near, i % 2, jnp.where(z > near, 1, 0))
        return jnp.where(below == 1, z - k, z + k), below

    def place(i, dy):
        zi = item(i)[0] if i else z
        return zi * 2 + (1 - y if dy else y)

    def relay(p, i, dy, dx):
        order = parts[p][3]
        far = {"z": i, "y": dy, "x": dx}
        came = max([n for n, axis in enumerate(order) if far[axis]], default=-1)
        b, f = place(i, dy), feat_x if dx else feat
        if came >= 0:
            arrive(p, b, f)
        ahead = order[came + 1:]
        if came >= 0 and order[came] == "z":
            below = item(i)[1]
            send(p, b, f, (blk + 2, feat), jnp.logical_and(below == 1, has_up))
            send(p, b, f, (blk - 2, feat), jnp.logical_and(below == 0, has_down))
        for axis in ahead:
            if axis == "z":
                send(p, b, f, (blk + 2, feat), has_up)
                send(p, b, f, (blk - 2, feat), has_down)
            else:
                send(p, b, f, (blk, feat_x) if axis == "x" else (blk_y, feat))
        send(p, b, f, (blk, feat_c))

    scale, bias = scale_ref[0], bias_ref[0]

    def unpack(b):
        for t in (0, 1):
            for q in range(-(-rows // GROUP)):
                n = min(GROUP, rows - q * GROUP)
                for f in range(4):
                    rbuf[t, b, q * GROUP:q * GROUP + n, f * rem:(f + 1) * rem] = (
                        buf[t, b, f, rows:rows + n, q * rem:(q + 1) * rem])

    def work(b):
        for t, u in ((0, 1), (1, 0)):
            dots = dot_nt(rbuf[t, blk], rbuf[u, b])
            for f in range(4):
                dots += dot_nt(buf[t, blk, f, 0:rows, :], buf[u, b, f, 0:rows, :])
            logit = scale * dots + bias
            r = lax.broadcasted_iota(jnp.int32, logit.shape, 0)
            col = lax.broadcasted_iota(jnp.int32, logit.shape, 1) + (b - blk) * rows
            diag = r == col
            value = jax.nn.sigmoid(jnp.where(diag, -logit, logit))
            slope = jnp.where(diag, -value, value).astype(BF16)
            acc[t] += jnp.dot(slope, buf[u, b, feat, 0:rows, :], preferred_element_type=F32)
            accr[t] += jnp.dot(slope, rbuf[u, b], preferred_element_type=F32)

    def finish(i, dy):
        b = place(i, dy)
        for p in range(len(parts)):
            for f in (feat_c, feat_xc):
                arrive(p, b, f)
        if i == 0 and dy == 0:
            acc[...] = jnp.zeros_like(acc)
            accr[...] = jnp.zeros_like(accr)
        unpack(b)
        work(b)

    events = []
    for i in range(nz):
        for dy in (0, 1):
            for dx in (0, 1):
                for p in range(len(parts)):
                    events.append((i + dy + dx, len(events), relay, (p, i, dy, dx)))
            events.append((i + dy + 3, len(events), finish, (i, dy)))
    for _, _, run, args in sorted(events, key=lambda event: event[:2]):
        run(*args)

    for t, ref in ((0, gi_ref), (1, gt_ref)):
        ref[:, 0:wide] = acc[t]
        for f in range(4):
            @pl.when(feat == f)
            def _():
                ref[:, wide:wide + rem] = accr[t, :, f * rem:(f + 1) * rem]

    for sid, (p, b, f, to, cond) in enumerate(sent):
        if cond is None:
            copy(p, b, f, to, sid).wait_send()
        else:
            @pl.when(cond)
            def _():
                copy(p, b, f, to, sid).wait_send()


def gathered(blocks, image, text, scale, bias):
    rows, width = image.shape
    wide = width // 128 * 128
    rem = width - wide
    nz = blocks // 2
    out = jax.ShapeDtypeStruct((rows, width), F32)
    image_sum, text_sum = pl.pallas_call(
        functools.partial(kernel, nz, rows, wide, rem),
        out_shape=(out, out),
        in_specs=[pl.BlockSpec(memory_space=pltpu.HBM)] * 2
        + [pl.BlockSpec(memory_space=pltpu.SMEM)] * 2,
        out_specs=(pl.BlockSpec(memory_space=pltpu.VMEM),) * 2,
        scratch_shapes=[
            pltpu.VMEM((2, rows, width), BF16),
            pltpu.SemaphoreType.DMA((2,)),
            pltpu.VMEM((2, blocks, 4, rows + GROUP, wide), BF16),
            pltpu.VMEM((2, blocks, rows, 4 * rem), BF16),
            pltpu.VMEM((2, rows, wide), F32),
            pltpu.VMEM((2, rows, 4 * rem), F32),
            pltpu.SemaphoreType.DMA((44 * nz,)),
            pltpu.SemaphoreType.DMA((4, blocks, 4)),
        ],
        compiler_params=pltpu.CompilerParams(
            collective_id=0, has_side_effects=True, vmem_limit_bytes=121 * 2**19
        ),
    )(image, text, scale.reshape(1), bias.reshape(1))
    return scale * image_sum, scale * text_sum


def solution(mesh):
    in_specs = (P("blk", "feat"), P("blk", "feat"), P(), P())
    out_specs = (P("blk", "feat"), P("blk", "feat"))
    blocks, feats = mesh.shape["blk"], mesh.shape["feat"]

    def body(image, text, scale, bias):
        whole = 2 * blocks * feats * image.size * 2
        if feats == 4 and blocks % 2 == 0 and whole <= 16 * 2**20:
            return gathered(blocks, image, text, scale, bias)
        return shards(image, text, scale, bias)

    return jax.shard_map(body, mesh=mesh, in_specs=in_specs, out_specs=out_specs, check_vma=False)
```

```python
import functools
import jax
import jax.numpy as jnp
from jax import lax
from jax.experimental import pallas as pl
from jax.experimental.pallas import tpu as pltpu
from jax.sharding import PartitionSpec as P


def from_behind(block, axis, distance):
    devices = range(lax.axis_size(axis))
    route = [((i - distance) % len(devices), i) for i in devices]
    return lax.ppermute(block, axis, route)


def pair_grads(image_all, current, scale, bias, diag_start, own):
    dots = lax.dot_general(
        image_all, current, (((1,), (1,)), ((), ())), preferred_element_type=jnp.float32
    )
    logit = scale * dots + bias
    if own:
        row_index = lax.broadcasted_iota(jnp.int32, logit.shape, 0)
        col_index = diag_start + lax.broadcasted_iota(jnp.int32, logit.shape, 1)
        value = jnp.where(row_index == col_index, -jax.nn.sigmoid(-logit), jax.nn.sigmoid(logit))
    else:
        value = jax.nn.sigmoid(logit)
    slope = value.astype(jnp.bfloat16)
    image_add = jnp.dot(slope, current, preferred_element_type=jnp.float32)
    text_add = lax.dot_general(
        slope, image_all, (((0,), (0,)), ((), ())), preferred_element_type=jnp.float32
    )
    return (image_add, text_add)


def pass_both(current, accum):
    return (
        from_behind(current.astype(jnp.float32), "blk", 1).astype(current.dtype),
        from_behind(accum, "blk", 1),
    )


def shards(image, text, scale, bias):
    block_count = lax.axis_size("blk")
    image_all = lax.all_gather(image, "feat", axis=1, tiled=True)
    quarter = lax.all_to_all(text, "feat", split_axis=0, concat_axis=1, tiled=True)
    rows_q = quarter.shape[0]
    diag_start = lax.axis_index("feat") * rows_q
    image_acc, text_acc = pair_grads(image_all, quarter, scale, bias, diag_start, True)

    def visit(step, carry):
        current, accum, grad_img = carry
        current, accum = pass_both(current, accum)
        image_add, text_add = pair_grads(image_all, current, scale, bias, 0, False)
        return (current, accum + text_add, grad_img + image_add)

    current, text_acc, image_acc = lax.fori_loop(
        1, block_count, visit, (quarter, text_acc, image_acc)
    )
    text_acc = from_behind(text_acc, "blk", 1)
    image_grad = scale * lax.psum_scatter(image_acc, "feat", scatter_dimension=1, tiled=True)
    text_grad = lax.all_to_all(scale * text_acc, "feat", split_axis=1, concat_axis=0, tiled=True)
    return (image_grad, text_grad)


MESH = pl.DeviceIdType.MESH
BF16 = jnp.bfloat16
F32 = jnp.float32
GROUP = 32


def round_up(value, unit):
    return -(-value // unit) * unit


def dot_nt(a, b):
    return lax.dot_general(a, b, (((1,), (1,)), ((), ())), preferred_element_type=F32)


def kernel(nz, rows, wide, rem, img_ref, txt_ref, scale_ref, bias_ref, gi_ref, gt_ref,
           own_in, in_sem, buf, slope_buf, mine, theirs, own_rem, acc, accr,
           ssem, rsem, slope_ssem, slope_rsem):
    blk, feat = lax.axis_index("blk"), lax.axis_index("feat")
    z, y = blk // 2, blk % 2
    x, c = feat // 2, feat % 2
    u = 1 - c
    blk_y = z * 2 + 1 - y
    feat_x = (1 - x) * 2 + c
    feat_c = x * 2 + 1 - c
    feat_xc = (1 - x) * 2 + 1 - c
    near = jnp.minimum(z, nz - 1 - z)
    groups = -(-rows // GROUP)
    cut = (rows + GROUP) * 5 // 8 // 16 * 16
    ranges = ((0, cut), (cut, rows + GROUP - cut))
    orders = (("zyx", "zxy"), ("yzx", "xzy"))

    def item(i):
        k = jnp.where(i <= 2 * near, (i + 1) // 2, i - near)
        below = jnp.where(i <= 2 * near, i % 2, jnp.where(z > near, 1, 0))
        return jnp.where(below == 1, z - k, z + k)

    planes = [z] + [item(i) for i in range(1, nz)]

    def place(i, dy):
        return planes[i] * 2 + (1 - y if dy else y)

    loads = [pltpu.make_async_copy(ref, own_in.at[t], in_sem.at[t])
             for t, ref in enumerate((img_ref, txt_ref))]
    for load in loads:
        load.start()

    barrier = pltpu.get_barrier_semaphore()
    for to in [(blk_y, feat), (blk, feat_x), (blk, feat_c)] + [
            (place(i, 0), feat) for i in range(1, nz)]:
        pl.semaphore_signal(barrier, inc=1, device_id=to, device_id_type=MESH)

    for t in (0, 1):
        loads[t].wait()
        buf[t, blk, feat, 0:rows, :] = own_in[t, :, 0:wide]
        last = own_in[t, :, wide:wide + rem]
        for q in range(groups):
            n = min(GROUP, rows - q * GROUP)
            buf[t, blk, feat, rows:rows + n, q * rem:(q + 1) * rem] = last[q * GROUP:q * GROUP + n]

    pl.semaphore_wait(barrier, 3 + nz - 1)

    sent = []

    def copy(h, t, b, f, to, sid):
        slot = buf.at[t, b, f, pl.ds(*ranges[h])]
        return pltpu.make_async_remote_copy(
            src_ref=slot, dst_ref=slot, send_sem=ssem.at[sid], recv_sem=rsem.at[h, t, b, f],
            device_id=to, device_id_type=MESH,
        )

    def send(h, t, b, f, to, cond=None):
        sid = len(sent)
        sent.append((h, t, b, f, to, cond))
        if cond is None:
            copy(h, t, b, f, to, sid).start()
        else:
            @pl.when(cond)
            def _():
                copy(h, t, b, f, to, sid).start()

    def wait_sent():
        for sid, (h, t, b, f, to, cond) in enumerate(sent):
            if cond is None:
                copy(h, t, b, f, to, sid).wait_send()
            else:
                @pl.when(cond)
                def _():
                    copy(h, t, b, f, to, sid).wait_send()

    def arrive(h, t, b, f):
        copy(h, t, b, f, (blk, feat_c), 0).wait_recv()

    def relay(h, t, i, dy, dx):
        order = orders[h][t]
        far = {"z": i, "y": dy, "x": dx}
        came = max([n for n, axis in enumerate(order) if far[axis]], default=-1)
        b, f = place(i, dy), feat_x if dx else feat
        if came >= 0:
            arrive(h, t, b, f)
        for axis in order[came + 1:]:
            if axis == "z":
                for other in range(1, nz):
                    send(h, t, b, f, (planes[other] * 2 + y, feat))
            else:
                send(h, t, b, f, (blk, feat_x) if axis == "x" else (blk_y, feat))
        send(h, t, b, f, (blk, feat_c), None if i == 0 and dy == 0 else c == t)

    scale, bias = scale_ref[0], bias_ref[0]

    def unpack(out, t, b):
        for q in range(groups):
            n = min(GROUP, rows - q * GROUP)
            for f in range(4):
                out[q * GROUP:q * GROUP + n, f * rem:(f + 1) * rem] = (
                    buf[t, b, f, rows:rows + n, q * rem:(q + 1) * rem])

    def hand(b):
        return pltpu.make_async_remote_copy(
            src_ref=slope_buf.at[c, b], dst_ref=slope_buf.at[c, b],
            send_sem=slope_ssem.at[b], recv_sem=slope_rsem.at[b],
            device_id=(blk, feat_c), device_id_type=MESH,
        )

    def finish(i, dy):
        b = place(i, dy)
        for h in (0, 1):
            for f in (feat_c, feat_xc):
                arrive(h, u, b, f)
                if i == 0 and dy == 0:
                    arrive(h, c, b, f)
        if i == 0 and dy == 0:
            unpack(mine, c, b)
            acc[...] = jnp.zeros_like(acc)
            accr[...] = jnp.zeros_like(accr)
        unpack(theirs, u, b)
        dots = dot_nt(mine[...], theirs[...])
        for f in range(4):
            dots += dot_nt(buf[c, blk, f, 0:rows, :], buf[u, b, f, 0:rows, :])
        logit = scale * dots + bias
        if i == 0 and dy == 0:
            diag = (lax.broadcasted_iota(jnp.int32, logit.shape, 0)
                    == lax.broadcasted_iota(jnp.int32, logit.shape, 1))
            value = jax.nn.sigmoid(jnp.where(diag, -logit, logit))
            value = jnp.where(diag, -value, value)
        else:
            value = jax.nn.sigmoid(logit)
        slope_buf[c, b] = value.astype(BF16)
        hand(b).start()

    def apply(i, dy):
        b = place(i, dy)
        for t in (0, 1):
            for q in range(groups):
                n = min(GROUP, rows - q * GROUP)
                own_rem[t, q * GROUP:q * GROUP + n, :] = (
                    buf[t, b, feat, rows:rows + n, q * rem:(q + 1) * rem])
        pltpu.make_async_remote_copy(
            src_ref=slope_buf.at[u, b], dst_ref=slope_buf.at[u, b],
            send_sem=slope_ssem.at[b], recv_sem=slope_rsem.at[b],
            device_id=(blk, feat_c), device_id_type=MESH,
        ).wait_recv()
        for t in (0, 1):
            slope = slope_buf[t, b]
            acc[t] += jnp.dot(slope, buf[1 - t, b, feat, 0:rows, :], preferred_element_type=F32)
            accr[t] += jnp.dot(slope, own_rem[1 - t], preferred_element_type=F32)

    events = []
    for i in range(nz):
        for dy in (0, 1):
            for dx in (0, 1):
                for h in (0, 1):
                    for t in (0, 1):
                        events.append((i + dy + dx, len(events), relay, (h, t, i, dy, dx)))
            events.append((i + dy + 2.5, len(events), finish, (i, dy)))
            events.append((i + dy + 3.6, len(events), apply, (i, dy)))
    events.append((nz + 2.4, len(events), wait_sent, ()))
    for _, _, run, args in sorted(events, key=lambda event: event[:2]):
        run(*args)

    for t, ref in ((0, gi_ref), (1, gt_ref)):
        ref[:, 0:wide] = scale * acc[t]
        ref[:, wide:wide + rem] = scale * accr[t]
    for b in range(nz * 2):
        hand(b).wait_send()


def gathered(blocks, image, text, scale, bias):
    rows, width = image.shape
    wide = width // 128 * 128
    rem = width - wide
    nz = blocks // 2
    out = jax.ShapeDtypeStruct((rows, width), F32)
    return pl.pallas_call(
        functools.partial(kernel, nz, rows, wide, rem),
        out_shape=(out, out),
        in_specs=[pl.BlockSpec(memory_space=pl.ANY)] * 2
        + [pl.BlockSpec(memory_space=pltpu.SMEM)] * 2,
        out_specs=(pl.BlockSpec(memory_space=pltpu.VMEM),) * 2,
        scratch_shapes=[
            pltpu.VMEM((2, rows, width), BF16),
            pltpu.SemaphoreType.DMA((2,)),
            pltpu.VMEM((2, blocks, 4, rows + GROUP, wide), BF16),
            pltpu.VMEM((2, blocks, rows, rows), BF16),
            pltpu.VMEM((rows, 4 * rem), BF16),
            pltpu.VMEM((rows, 4 * rem), BF16),
            pltpu.VMEM((2, rows, rem), BF16),
            pltpu.VMEM((2, rows, wide), F32),
            pltpu.VMEM((2, rows, rem), F32),
            pltpu.SemaphoreType.DMA((44 * nz,)),
            pltpu.SemaphoreType.DMA((2, 2, blocks, 4)),
            pltpu.SemaphoreType.DMA((blocks,)),
            pltpu.SemaphoreType.DMA((blocks,)),
        ],
        compiler_params=pltpu.CompilerParams(
            collective_id=0, has_side_effects=True, vmem_limit_bytes=48 * 2**20
        ),
    )(image, text, scale.reshape(1), bias.reshape(1))


def solution(mesh):
    in_specs = (P("blk", "feat"), P("blk", "feat"), P(), P())
    out_specs = (P("blk", "feat"), P("blk", "feat"))
    blocks, feats = mesh.shape["blk"], mesh.shape["feat"]

    def body(image, text, scale, bias):
        whole = 2 * blocks * feats * image.size * 2
        if feats == 4 and blocks % 2 == 0 and whole <= 16 * 2**20:
            return gathered(blocks, image, text, scale, bias)
        return shards(image, text, scale, bias)

    return jax.shard_map(body, mesh=mesh, in_specs=in_specs, out_specs=out_specs, check_vma=False)
```

```python
import functools
import jax
import jax.numpy as jnp
from jax import lax
from jax.experimental import pallas as pl
from jax.experimental.pallas import tpu as pltpu
from jax.sharding import PartitionSpec as P


def from_behind(block, axis, distance):
    devices = range(lax.axis_size(axis))
    route = [((i - distance) % len(devices), i) for i in devices]
    return lax.ppermute(block, axis, route)


def pair_grads(image_all, current, scale, bias, diag_start, own):
    dots = lax.dot_general(
        image_all, current, (((1,), (1,)), ((), ())), preferred_element_type=jnp.float32
    )
    logit = scale * dots + bias
    if own:
        row_index = lax.broadcasted_iota(jnp.int32, logit.shape, 0)
        col_index = diag_start + lax.broadcasted_iota(jnp.int32, logit.shape, 1)
        value = jnp.where(row_index == col_index, -jax.nn.sigmoid(-logit), jax.nn.sigmoid(logit))
    else:
        value = jax.nn.sigmoid(logit)
    slope = value.astype(jnp.bfloat16)
    image_add = jnp.dot(slope, current, preferred_element_type=jnp.float32)
    text_add = lax.dot_general(
        slope, image_all, (((0,), (0,)), ((), ())), preferred_element_type=jnp.float32
    )
    return (image_add, text_add)


def pass_both(current, accum):
    return (
        from_behind(current.astype(jnp.float32), "blk", 1).astype(current.dtype),
        from_behind(accum, "blk", 1),
    )


def shards(image, text, scale, bias):
    block_count = lax.axis_size("blk")
    image_all = lax.all_gather(image, "feat", axis=1, tiled=True)
    quarter = lax.all_to_all(text, "feat", split_axis=0, concat_axis=1, tiled=True)
    rows_q = quarter.shape[0]
    diag_start = lax.axis_index("feat") * rows_q
    image_acc, text_acc = pair_grads(image_all, quarter, scale, bias, diag_start, True)

    def visit(step, carry):
        current, accum, grad_img = carry
        current, accum = pass_both(current, accum)
        image_add, text_add = pair_grads(image_all, current, scale, bias, 0, False)
        return (current, accum + text_add, grad_img + image_add)

    current, text_acc, image_acc = lax.fori_loop(
        1, block_count, visit, (quarter, text_acc, image_acc)
    )
    text_acc = from_behind(text_acc, "blk", 1)
    image_grad = scale * lax.psum_scatter(image_acc, "feat", scatter_dimension=1, tiled=True)
    text_grad = lax.all_to_all(scale * text_acc, "feat", split_axis=1, concat_axis=0, tiled=True)
    return (image_grad, text_grad)


MESH = pl.DeviceIdType.MESH
BF16 = jnp.bfloat16
F32 = jnp.float32
GROUP = 32


def round_up(value, unit):
    return -(-value // unit) * unit


def dot_nt(a, b):
    return lax.dot_general(a, b, (((1,), (1,)), ((), ())), preferred_element_type=F32)


def kernel(nz, rows, wide, rem, img_ref, txt_ref, scale_ref, bias_ref, gi_ref, gt_ref,
           own_in, in_sem, buf, slope_buf, mine, theirs, own_rem, acc, accr,
           ssem, rsem, slope_ssem, slope_rsem):
    blk, feat = lax.axis_index("blk"), lax.axis_index("feat")
    z, y = blk // 2, blk % 2
    x, c = feat // 2, feat % 2
    u = 1 - c
    blk_y = z * 2 + 1 - y
    feat_x = (1 - x) * 2 + c
    feat_c = x * 2 + 1 - c
    feat_xc = (1 - x) * 2 + 1 - c
    near = jnp.minimum(z, nz - 1 - z)
    groups = -(-rows // GROUP)
    cut = (rows + GROUP) * 2 // 5 // 16 * 16
    has_up, has_down = z < nz - 1, z > 0
    ranges = ((0, cut), (cut, rows + GROUP - cut))
    orders = (("zyx", "zxy"), ("yzx", "xzy"))

    def item(i):
        k = jnp.where(i <= 2 * near, (i + 1) // 2, i - near)
        below = jnp.where(i <= 2 * near, i % 2, jnp.where(z > near, 1, 0))
        return jnp.where(below == 1, z - k, z + k)

    planes = [z] + [item(i) for i in range(1, nz)]

    def along_z(act):
        @pl.when(has_up)
        def _():
            act((blk + 2, feat))

        @pl.when(has_down)
        def _():
            act((blk - 2, feat))

    def place(i, dy):
        return planes[i] * 2 + (1 - y if dy else y)

    loads = [pltpu.make_async_copy(ref, own_in.at[t], in_sem.at[t])
             for t, ref in enumerate((img_ref, txt_ref))]
    for load in loads:
        load.start()

    barrier = pltpu.get_barrier_semaphore()

    def greet(to):
        pl.semaphore_signal(barrier, inc=1, device_id=to, device_id_type=MESH)

    for to in ((blk_y, feat), (blk, feat_x), (blk, feat_c)):
        greet(to)
    along_z(greet)

    for t in (0, 1):
        loads[t].wait()
        buf[t, blk, feat, 0:rows, :] = own_in[t, :, 0:wide]
        last = own_in[t, :, wide:wide + rem]
        for q in range(groups):
            n = min(GROUP, rows - q * GROUP)
            buf[t, blk, feat, rows:rows + n, q * rem:(q + 1) * rem] = last[q * GROUP:q * GROUP + n]

    pl.semaphore_wait(barrier, 3 + jnp.where(has_up, 1, 0) + jnp.where(has_down, 1, 0))

    sent = []

    def copy(h, t, b, f, to, sid):
        slot = buf.at[t, b, f, pl.ds(*ranges[h])]
        return pltpu.make_async_remote_copy(
            src_ref=slot, dst_ref=slot, send_sem=ssem.at[sid], recv_sem=rsem.at[h, t, b, f],
            device_id=to, device_id_type=MESH,
        )

    def send(h, t, b, f, to, cond=None):
        sid = len(sent)
        sent.append((h, t, b, f, to, cond))
        if cond is None:
            copy(h, t, b, f, to, sid).start()
        else:
            @pl.when(cond)
            def _():
                copy(h, t, b, f, to, sid).start()

    def wait_sent():
        for sid, (h, t, b, f, to, cond) in enumerate(sent):
            if cond is None:
                copy(h, t, b, f, to, sid).wait_send()
            else:
                @pl.when(cond)
                def _():
                    copy(h, t, b, f, to, sid).wait_send()

    def arrive(h, t, b, f):
        copy(h, t, b, f, (blk, feat_c), 0).wait_recv()

    def relay(h, t, i, dy, dx):
        order = orders[h][t]
        far = {"z": i, "y": dy, "x": dx}
        came = max([n for n, axis in enumerate(order) if far[axis]], default=-1)
        b, f = place(i, dy), feat_x if dx else feat
        if came >= 0:
            arrive(h, t, b, f)
        if i and order[came] == "z":
            send(h, t, b, f, (blk + 2, feat), jnp.logical_and(planes[i] < z, has_up))
            send(h, t, b, f, (blk - 2, feat), jnp.logical_and(planes[i] > z, has_down))
        for axis in order[came + 1:]:
            if axis == "z":
                send(h, t, b, f, (blk + 2, feat), has_up)
                send(h, t, b, f, (blk - 2, feat), has_down)
            else:
                send(h, t, b, f, (blk, feat_x) if axis == "x" else (blk_y, feat))
        send(h, t, b, f, (blk, feat_c), None if i == 0 and dy == 0 else c == t)

    scale, bias = scale_ref[0], bias_ref[0]

    def unpack(out, t, b):
        for q in range(groups):
            n = min(GROUP, rows - q * GROUP)
            for f in range(4):
                out[q * GROUP:q * GROUP + n, f * rem:(f + 1) * rem] = (
                    buf[t, b, f, rows:rows + n, q * rem:(q + 1) * rem])

    def hand(b):
        return pltpu.make_async_remote_copy(
            src_ref=slope_buf.at[c, b], dst_ref=slope_buf.at[c, b],
            send_sem=slope_ssem.at[b], recv_sem=slope_rsem.at[b],
            device_id=(blk, feat_c), device_id_type=MESH,
        )

    def finish(i, dy):
        b = place(i, dy)
        for h in (0, 1):
            for f in (feat_c, feat_xc):
                arrive(h, u, b, f)
                if i == 0 and dy == 0:
                    arrive(h, c, b, f)
        if i == 0 and dy == 0:
            unpack(mine, c, b)
            acc[...] = jnp.zeros_like(acc)
            accr[...] = jnp.zeros_like(accr)
        unpack(theirs, u, b)
        dots = dot_nt(mine[...], theirs[...])
        for f in range(4):
            dots += dot_nt(buf[c, blk, f, 0:rows, :], buf[u, b, f, 0:rows, :])
        logit = scale * dots + bias
        if i == 0 and dy == 0:
            diag = (lax.broadcasted_iota(jnp.int32, logit.shape, 0)
                    == lax.broadcasted_iota(jnp.int32, logit.shape, 1))
            value = jax.nn.sigmoid(jnp.where(diag, -logit, logit))
            value = jnp.where(diag, -value, value)
        else:
            value = jax.nn.sigmoid(logit)
        slope_buf[c, b] = value.astype(BF16)
        hand(b).start()

    def apply(i, dy):
        b = place(i, dy)
        for t in (0, 1):
            for q in range(groups):
                n = min(GROUP, rows - q * GROUP)
                own_rem[t, q * GROUP:q * GROUP + n, :] = (
                    buf[t, b, feat, rows:rows + n, q * rem:(q + 1) * rem])
        pltpu.make_async_remote_copy(
            src_ref=slope_buf.at[u, b], dst_ref=slope_buf.at[u, b],
            send_sem=slope_ssem.at[b], recv_sem=slope_rsem.at[b],
            device_id=(blk, feat_c), device_id_type=MESH,
        ).wait_recv()
        for t in (0, 1):
            slope = slope_buf[t, b]
            acc[t] += jnp.dot(slope, buf[1 - t, b, feat, 0:rows, :], preferred_element_type=F32)
            accr[t] += jnp.dot(slope, own_rem[1 - t], preferred_element_type=F32)

    events = []
    for i in range(nz):
        for dy in (0, 1):
            for dx in (0, 1):
                for h in (0, 1):
                    for t in (0, 1):
                        events.append((i + dy + dx, len(events), relay, (h, t, i, dy, dx)))
            events.append((i + dy + 2.5, len(events), finish, (i, dy)))
            events.append((i + dy + 3.6, len(events), apply, (i, dy)))
    events.append((nz + 2.4, len(events), wait_sent, ()))
    for _, _, run, args in sorted(events, key=lambda event: event[:2]):
        run(*args)

    for t, ref in ((0, gi_ref), (1, gt_ref)):
        ref[:, 0:wide] = scale * acc[t]
        ref[:, wide:wide + rem] = scale * accr[t]
    for b in range(nz * 2):
        hand(b).wait_send()


def gathered(blocks, image, text, scale, bias):
    rows, width = image.shape
    wide = width // 128 * 128
    rem = width - wide
    nz = blocks // 2
    out = jax.ShapeDtypeStruct((rows, width), F32)
    return pl.pallas_call(
        functools.partial(kernel, nz, rows, wide, rem),
        out_shape=(out, out),
        in_specs=[pl.BlockSpec(memory_space=pl.ANY)] * 2
        + [pl.BlockSpec(memory_space=pltpu.SMEM)] * 2,
        out_specs=(pl.BlockSpec(memory_space=pltpu.VMEM),) * 2,
        scratch_shapes=[
            pltpu.VMEM((2, rows, width), BF16),
            pltpu.SemaphoreType.DMA((2,)),
            pltpu.VMEM((2, blocks, 4, rows + GROUP, wide), BF16),
            pltpu.VMEM((2, blocks, rows, rows), BF16),
            pltpu.VMEM((rows, 4 * rem), BF16),
            pltpu.VMEM((rows, 4 * rem), BF16),
            pltpu.VMEM((2, rows, rem), BF16),
            pltpu.VMEM((2, rows, wide), F32),
            pltpu.VMEM((2, rows, rem), F32),
            pltpu.SemaphoreType.DMA((44 * nz,)),
            pltpu.SemaphoreType.DMA((2, 2, blocks, 4)),
            pltpu.SemaphoreType.DMA((blocks,)),
            pltpu.SemaphoreType.DMA((blocks,)),
        ],
        compiler_params=pltpu.CompilerParams(
            collective_id=0, has_side_effects=True, vmem_limit_bytes=48 * 2**20
        ),
    )(image, text, scale.reshape(1), bias.reshape(1))


def solution(mesh):
    in_specs = (P("blk", "feat"), P("blk", "feat"), P(), P())
    out_specs = (P("blk", "feat"), P("blk", "feat"))
    blocks, feats = mesh.shape["blk"], mesh.shape["feat"]

    def body(image, text, scale, bias):
        whole = 2 * blocks * feats * image.size * 2
        if feats == 4 and blocks % 2 == 0 and whole <= 16 * 2**20:
            return gathered(blocks, image, text, scale, bias)
        return shards(image, text, scale, bias)

    return jax.shard_map(body, mesh=mesh, in_specs=in_specs, out_specs=out_specs, check_vma=False)
```

```python
import functools
import jax
import jax.numpy as jnp
from jax import lax
from jax.experimental import pallas as pl
from jax.experimental.pallas import tpu as pltpu
from jax.sharding import PartitionSpec as P


def from_behind(block, axis, distance):
    devices = range(lax.axis_size(axis))
    route = [((i - distance) % len(devices), i) for i in devices]
    return lax.ppermute(block, axis, route)


def pair_grads(image_all, current, scale, bias, diag_start, own):
    dots = lax.dot_general(
        image_all, current, (((1,), (1,)), ((), ())), preferred_element_type=jnp.float32
    )
    logit = scale * dots + bias
    if own:
        row_index = lax.broadcasted_iota(jnp.int32, logit.shape, 0)
        col_index = diag_start + lax.broadcasted_iota(jnp.int32, logit.shape, 1)
        value = jnp.where(row_index == col_index, -jax.nn.sigmoid(-logit), jax.nn.sigmoid(logit))
    else:
        value = jax.nn.sigmoid(logit)
    slope = value.astype(jnp.bfloat16)
    image_add = jnp.dot(slope, current, preferred_element_type=jnp.float32)
    text_add = lax.dot_general(
        slope, image_all, (((0,), (0,)), ((), ())), preferred_element_type=jnp.float32
    )
    return (image_add, text_add)


def pass_both(current, accum):
    return (
        from_behind(current.astype(jnp.float32), "blk", 1).astype(current.dtype),
        from_behind(accum, "blk", 1),
    )


def shards(image, text, scale, bias):
    block_count = lax.axis_size("blk")
    image_all = lax.all_gather(image, "feat", axis=1, tiled=True)
    quarter = lax.all_to_all(text, "feat", split_axis=0, concat_axis=1, tiled=True)
    rows_q = quarter.shape[0]
    diag_start = lax.axis_index("feat") * rows_q
    image_acc, text_acc = pair_grads(image_all, quarter, scale, bias, diag_start, True)

    def visit(step, carry):
        current, accum, grad_img = carry
        current, accum = pass_both(current, accum)
        image_add, text_add = pair_grads(image_all, current, scale, bias, 0, False)
        return (current, accum + text_add, grad_img + image_add)

    current, text_acc, image_acc = lax.fori_loop(
        1, block_count, visit, (quarter, text_acc, image_acc)
    )
    text_acc = from_behind(text_acc, "blk", 1)
    image_grad = scale * lax.psum_scatter(image_acc, "feat", scatter_dimension=1, tiled=True)
    text_grad = lax.all_to_all(scale * text_acc, "feat", split_axis=1, concat_axis=0, tiled=True)
    return (image_grad, text_grad)


MESH = pl.DeviceIdType.MESH
BF16 = jnp.bfloat16
F32 = jnp.float32
STEPS = (
    (
        0, 16, 32, 2, 17, 48, 1, 4, 34, 33, 20, 50, 8, 49, 19, 18, 52, 35, 22, 36,
        64, 24, 53, 40, 25, 9, 10, 51, 56, 21, 38, 27, 3, 6, 11, 37, 41, 54, 12, 128,
        55, 28, 66, 42, 5, 14, 57, 44, 60, 29, 30, 39, 58, 23, 26, 68, 59, 61, 43, 13,
        7, 72, 45, 46, 130, 15, 31, 74, 62, 76, 63, 47, 70, 136, 138, 78, 140, 132, 134, 142,
    ),
    (
        48, 0, 32, 16, 2, 1, 4, 50, 8, 34, 20, 49, 18, 24, 33, 17, 40, 36, 56, 52,
        35, 9, 51, 5, 3, 22, 12, 38, 6, 19, 28, 64, 44, 26, 53, 42, 57, 21, 25, 39,
        58, 37, 60, 54, 66, 10, 41, 61, 55, 14, 68, 7, 46, 23, 72, 59, 27, 43, 13, 45,
        70, 11, 30, 62, 29, 136, 15, 74, 76, 47, 31, 63, 128, 132, 130, 78, 134, 138, 140, 142,
    ),
)
PLANES = 4
GROUP = 32


def round_up(value, unit):
    return -(-value // unit) * unit


def dot_nt(a, b):
    return lax.dot_general(a, b, (((1,), (1,)), ((), ())), preferred_element_type=F32)


def kernel(nz, rows, wide, rem, img_ref, txt_ref, scale_ref, bias_ref, gi_ref, gt_ref,
           own_in, in_sem, buf, slope_buf, mine, theirs, own_rem, acc, accr,
           ssem, rsem, slope_ssem, slope_rsem):
    blk, feat = lax.axis_index("blk"), lax.axis_index("feat")
    z, y = blk // 2, blk % 2
    x, c = feat // 2, feat % 2
    u = 1 - c
    blk_y = z * 2 + 1 - y
    feat_x = (1 - x) * 2 + c
    feat_c = x * 2 + 1 - c
    feat_xc = (1 - x) * 2 + 1 - c
    near = jnp.minimum(z, nz - 1 - z)
    groups = -(-rows // GROUP)
    cut = (rows + GROUP) * 5 // 13 // 16 * 16
    has_up, has_down = z < nz - 1, z > 0
    ranges = ((0, cut), (cut, rows + GROUP - cut))
    orders = (("zyx", "zxy"), ("yzx", "xzy"))

    def item(i):
        k = jnp.where(i <= 2 * near, (i + 1) // 2, i - near)
        below = jnp.where(i <= 2 * near, i % 2, jnp.where(z > near, 1, 0))
        return jnp.where(below == 1, z - k, z + k)

    planes = [z] + [item(i) for i in range(1, nz)]

    def along_z(act):
        @pl.when(has_up)
        def _():
            act((blk + 2, feat))

        @pl.when(has_down)
        def _():
            act((blk - 2, feat))

    def place(i, dy):
        return planes[i] * 2 + (1 - y if dy else y)

    loads = [pltpu.make_async_copy(ref, own_in.at[t], in_sem.at[t])
             for t, ref in enumerate((img_ref, txt_ref))]
    for load in loads:
        load.start()

    barrier = pltpu.get_barrier_semaphore()

    def greet(to):
        pl.semaphore_signal(barrier, inc=1, device_id=to, device_id_type=MESH)

    for to in ((blk_y, feat), (blk, feat_x), (blk, feat_c)):
        greet(to)
    along_z(greet)

    for t in (0, 1):
        loads[t].wait()
        buf[t, blk, feat, 0:rows, :] = own_in[t, :, 0:wide]
        last = own_in[t, :, wide:wide + rem]
        for q in range(groups):
            n = min(GROUP, rows - q * GROUP)
            buf[t, blk, feat, rows:rows + n, q * rem:(q + 1) * rem] = last[q * GROUP:q * GROUP + n]

    pl.semaphore_wait(barrier, 3 + jnp.where(has_up, 1, 0) + jnp.where(has_down, 1, 0))

    sent = []

    def copy(h, t, b, f, to, sid):
        slot = buf.at[t, b, f, pl.ds(*ranges[h])]
        return pltpu.make_async_remote_copy(
            src_ref=slot, dst_ref=slot, send_sem=ssem.at[sid], recv_sem=rsem.at[h, t, b, f],
            device_id=to, device_id_type=MESH,
        )

    def send(h, t, b, f, to, cond=None):
        sid = len(sent)
        sent.append((h, t, b, f, to, cond))
        if cond is None:
            copy(h, t, b, f, to, sid).start()
        else:
            @pl.when(cond)
            def _():
                copy(h, t, b, f, to, sid).start()

    def wait_sent():
        for sid, (h, t, b, f, to, cond) in enumerate(sent):
            if cond is None:
                copy(h, t, b, f, to, sid).wait_send()
            else:
                @pl.when(cond)
                def _():
                    copy(h, t, b, f, to, sid).wait_send()

    def arrive(h, t, b, f):
        copy(h, t, b, f, (blk, feat_c), 0).wait_recv()

    def relay(h, t, i, dy, dx):
        order = orders[h][t]
        far = {"z": i, "y": dy, "x": dx}
        came = max([n for n, axis in enumerate(order) if far[axis]], default=-1)
        b, f = place(i, dy), feat_x if dx else feat
        if came >= 0:
            arrive(h, t, b, f)
        if i and order[came] == "z":
            send(h, t, b, f, (blk + 2, feat), jnp.logical_and(planes[i] < z, has_up))
            send(h, t, b, f, (blk - 2, feat), jnp.logical_and(planes[i] > z, has_down))
        for axis in order[came + 1:]:
            if axis == "z":
                send(h, t, b, f, (blk + 2, feat), has_up)
                send(h, t, b, f, (blk - 2, feat), has_down)
            else:
                send(h, t, b, f, (blk, feat_x) if axis == "x" else (blk_y, feat))
        send(h, t, b, f, (blk, feat_c), None if i == 0 and dy == 0 else c == t)

    scale, bias = scale_ref[0], bias_ref[0]

    def unpack(out, t, b):
        for q in range(groups):
            n = min(GROUP, rows - q * GROUP)
            for f in range(4):
                out[q * GROUP:q * GROUP + n, f * rem:(f + 1) * rem] = (
                    buf[t, b, f, rows:rows + n, q * rem:(q + 1) * rem])

    def hand(b):
        return pltpu.make_async_remote_copy(
            src_ref=slope_buf.at[c, b], dst_ref=slope_buf.at[c, b],
            send_sem=slope_ssem.at[b], recv_sem=slope_rsem.at[b],
            device_id=(blk, feat_c), device_id_type=MESH,
        )

    def finish(i, dy):
        b = place(i, dy)
        for h in (0, 1):
            for f in (feat_c, feat_xc):
                arrive(h, u, b, f)
                if i == 0 and dy == 0:
                    arrive(h, c, b, f)
        if i == 0 and dy == 0:
            unpack(mine, c, b)
        unpack(theirs, u, b)
        dots = dot_nt(mine[...], theirs[...])
        for f in range(4):
            dots += dot_nt(buf[c, blk, f, 0:rows, :], buf[u, b, f, 0:rows, :])
        logit = scale * dots + bias
        if i == 0 and dy == 0:
            diag = (lax.broadcasted_iota(jnp.int32, logit.shape, 0)
                    == lax.broadcasted_iota(jnp.int32, logit.shape, 1))
            value = jax.nn.sigmoid(jnp.where(diag, -logit, logit))
            value = jnp.where(diag, -value, value)
        else:
            value = jax.nn.sigmoid(logit)
        slope_buf[c, b] = value.astype(BF16)
        hand(b).start()

    def apply(i, dy):
        b = place(i, dy)
        for t in (0, 1):
            for q in range(groups):
                n = min(GROUP, rows - q * GROUP)
                own_rem[t, q * GROUP:q * GROUP + n, :] = (
                    buf[t, b, feat, rows:rows + n, q * rem:(q + 1) * rem])
        pltpu.make_async_remote_copy(
            src_ref=slope_buf.at[u, b], dst_ref=slope_buf.at[u, b],
            send_sem=slope_ssem.at[b], recv_sem=slope_rsem.at[b],
            device_id=(blk, feat_c), device_id_type=MESH,
        ).wait_recv()
        for t in (0, 1):
            slope = slope_buf[t, b]
            acc[t] += jnp.dot(slope, buf[1 - t, b, feat, 0:rows, :], preferred_element_type=F32)
            accr[t] += jnp.dot(slope, own_rem[1 - t], preferred_element_type=F32)

    acc[...] = jnp.zeros_like(acc)
    accr[...] = jnp.zeros_like(accr)

    def steps(codes):
        sent.clear()
        slopes = 0
        for step in codes:
            kind, part, i, dy, dx = step // 64, step // 16 % 4, step // 4 % 4, step // 2 % 2, step % 2
            if kind == 0:
                relay(part // 2, part % 2, i, dy, dx)
            elif kind == 1:
                finish(i, dy)
                slopes += 1
                if slopes == 2 * nz:
                    wait_sent()
            else:
                apply(i, dy)

    for inner, codes in enumerate(STEPS):
        @pl.when((near > 0) == bool(inner))
        def _():
            steps(codes)

    for t, ref in ((0, gi_ref), (1, gt_ref)):
        ref[:, 0:wide] = scale * acc[t]
        ref[:, wide:wide + rem] = scale * accr[t]
    for b in range(nz * 2):
        hand(b).wait_send()


def gathered(blocks, image, text, scale, bias):
    rows, width = image.shape
    wide = width // 128 * 128
    rem = width - wide
    nz = blocks // 2
    out = jax.ShapeDtypeStruct((rows, width), F32)
    return pl.pallas_call(
        functools.partial(kernel, nz, rows, wide, rem),
        out_shape=(out, out),
        in_specs=[pl.BlockSpec(memory_space=pl.ANY)] * 2
        + [pl.BlockSpec(memory_space=pltpu.SMEM)] * 2,
        out_specs=(pl.BlockSpec(memory_space=pltpu.VMEM),) * 2,
        scratch_shapes=[
            pltpu.VMEM((2, rows, width), BF16),
            pltpu.SemaphoreType.DMA((2,)),
            pltpu.VMEM((2, blocks, 4, rows + GROUP, wide), BF16),
            pltpu.VMEM((2, blocks, rows, rows), BF16),
            pltpu.VMEM((rows, 4 * rem), BF16),
            pltpu.VMEM((rows, 4 * rem), BF16),
            pltpu.VMEM((2, rows, rem), BF16),
            pltpu.VMEM((2, rows, wide), F32),
            pltpu.VMEM((2, rows, rem), F32),
            pltpu.SemaphoreType.DMA((44 * nz,)),
            pltpu.SemaphoreType.DMA((2, 2, blocks, 4)),
            pltpu.SemaphoreType.DMA((blocks,)),
            pltpu.SemaphoreType.DMA((blocks,)),
        ],
        compiler_params=pltpu.CompilerParams(
            collective_id=0, has_side_effects=True, vmem_limit_bytes=48 * 2**20
        ),
    )(image, text, scale.reshape(1), bias.reshape(1))


def solution(mesh):
    in_specs = (P("blk", "feat"), P("blk", "feat"), P(), P())
    out_specs = (P("blk", "feat"), P("blk", "feat"))
    blocks, feats = mesh.shape["blk"], mesh.shape["feat"]

    def body(image, text, scale, bias):
        whole = 2 * blocks * feats * image.size * 2
        if feats == 4 and blocks == 2 * PLANES and whole <= 16 * 2**20:
            return gathered(blocks, image, text, scale, bias)
        return shards(image, text, scale, bias)

    return jax.shard_map(body, mesh=mesh, in_specs=in_specs, out_specs=out_specs, check_vma=False)
```

```python
import functools
import jax
import jax.numpy as jnp
from jax import lax
from jax.experimental import pallas as pl
from jax.experimental.pallas import tpu as pltpu
from jax.sharding import PartitionSpec as P


def from_behind(block, axis, distance):
    devices = range(lax.axis_size(axis))
    route = [((i - distance) % len(devices), i) for i in devices]
    return lax.ppermute(block, axis, route)


def pair_grads(image_all, current, scale, bias, diag_start, own):
    dots = lax.dot_general(
        image_all, current, (((1,), (1,)), ((), ())), preferred_element_type=jnp.float32
    )
    logit = scale * dots + bias
    if own:
        row_index = lax.broadcasted_iota(jnp.int32, logit.shape, 0)
        col_index = diag_start + lax.broadcasted_iota(jnp.int32, logit.shape, 1)
        value = jnp.where(row_index == col_index, -jax.nn.sigmoid(-logit), jax.nn.sigmoid(logit))
    else:
        value = jax.nn.sigmoid(logit)
    slope = value.astype(jnp.bfloat16)
    image_add = jnp.dot(slope, current, preferred_element_type=jnp.float32)
    text_add = lax.dot_general(
        slope, image_all, (((0,), (0,)), ((), ())), preferred_element_type=jnp.float32
    )
    return (image_add, text_add)


def pass_both(current, accum):
    return (
        from_behind(current.astype(jnp.float32), "blk", 1).astype(current.dtype),
        from_behind(accum, "blk", 1),
    )


def shards(image, text, scale, bias):
    block_count = lax.axis_size("blk")
    image_all = lax.all_gather(image, "feat", axis=1, tiled=True)
    quarter = lax.all_to_all(text, "feat", split_axis=0, concat_axis=1, tiled=True)
    rows_q = quarter.shape[0]
    diag_start = lax.axis_index("feat") * rows_q
    image_acc, text_acc = pair_grads(image_all, quarter, scale, bias, diag_start, True)

    def visit(step, carry):
        current, accum, grad_img = carry
        current, accum = pass_both(current, accum)
        image_add, text_add = pair_grads(image_all, current, scale, bias, 0, False)
        return (current, accum + text_add, grad_img + image_add)

    current, text_acc, image_acc = lax.fori_loop(
        1, block_count, visit, (quarter, text_acc, image_acc)
    )
    text_acc = from_behind(text_acc, "blk", 1)
    image_grad = scale * lax.psum_scatter(image_acc, "feat", scatter_dimension=1, tiled=True)
    text_grad = lax.all_to_all(scale * text_acc, "feat", split_axis=1, concat_axis=0, tiled=True)
    return (image_grad, text_grad)


MESH = pl.DeviceIdType.MESH
BF16 = jnp.bfloat16
F32 = jnp.float32
STEPS = (
    (
        16, 48, 0, 32, 17, 1, 2, 4, 49, 34, 19, 5, 6, 20, 35, 52, 8, 18, 51, 38,
        33, 36, 24, 3, 56, 50, 40, 37, 9, 21, 54, 58, 10, 42, 7, 53, 64, 12, 68, 11,
        25, 28, 26, 57, 39, 41, 44, 43, 55, 66, 22, 23, 60, 14, 72, 29, 130, 13, 30, 27,
        45, 46, 59, 15, 61, 132, 70, 74, 62, 128, 47, 63, 31, 134, 76, 78, 136, 140, 138, 142,
    ),
    (
        48, 32, 0, 16, 34, 49, 8, 2, 18, 4, 33, 1, 24, 56, 50, 20, 40, 52, 35, 5,
        36, 17, 10, 6, 3, 9, 58, 51, 38, 28, 42, 64, 54, 12, 53, 25, 44, 37, 57, 7,
        30, 21, 60, 19, 22, 26, 46, 41, 27, 55, 66, 39, 128, 61, 29, 11, 23, 43, 68, 13,
        59, 130, 14, 70, 63, 72, 45, 31, 62, 47, 74, 132, 15, 76, 136, 78, 134, 138, 140, 142,
    ),
)
PLANES = 4
GROUP = 32


def round_up(value, unit):
    return -(-value // unit) * unit


def dot_nt(a, b):
    return lax.dot_general(a, b, (((1,), (1,)), ((), ())), preferred_element_type=F32)


def kernel(nz, rows, wide, rem, img_ref, txt_ref, scale_ref, bias_ref, gi_ref, gt_ref,
           own_in, in_sem, buf, slope_buf, mine, theirs, own_rem, acc, accr,
           ssem, rsem, slope_ssem, slope_rsem):
    blk, feat = lax.axis_index("blk"), lax.axis_index("feat")
    z, y = blk // 2, blk % 2
    x, c = feat // 2, feat % 2
    u = 1 - c
    blk_y = z * 2 + 1 - y
    feat_x = (1 - x) * 2 + c
    feat_c = x * 2 + 1 - c
    feat_xc = (1 - x) * 2 + 1 - c
    near = jnp.minimum(z, nz - 1 - z)
    groups = -(-rows // GROUP)
    cut = (rows + GROUP) * 5 // 13 // 16 * 16
    has_up, has_down = z < nz - 1, z > 0
    ranges = ((0, cut), (cut, rows + GROUP - cut))
    orders = (("zyx", "zxy"), ("yzx", "xzy"))

    def item(i):
        k = jnp.where(i <= 2 * near, (i + 1) // 2, i - near)
        below = jnp.where(i <= 2 * near, i % 2, jnp.where(z > near, 1, 0))
        return jnp.where(below == 1, z - k, z + k)

    planes = [z] + [item(i) for i in range(1, nz)]

    def along_z(act):
        @pl.when(has_up)
        def _():
            act((blk + 2, feat))

        @pl.when(has_down)
        def _():
            act((blk - 2, feat))

    def place(i, dy):
        return planes[i] * 2 + (1 - y if dy else y)

    loads = [pltpu.make_async_copy(ref, own_in.at[t], in_sem.at[t])
             for t, ref in enumerate((img_ref, txt_ref))]
    for load in loads:
        load.start()

    barrier = pltpu.get_barrier_semaphore()

    def greet(to):
        pl.semaphore_signal(barrier, inc=1, device_id=to, device_id_type=MESH)

    for to in ((blk_y, feat), (blk, feat_x), (blk, feat_c)):
        greet(to)
    along_z(greet)

    for t in (0, 1):
        loads[t].wait()
        buf[t, blk, feat, 0:rows, :] = own_in[t, :, 0:wide]
        last = own_in[t, :, wide:wide + rem]
        for q in range(groups):
            n = min(GROUP, rows - q * GROUP)
            buf[t, blk, feat, rows:rows + n, q * rem:(q + 1) * rem] = last[q * GROUP:q * GROUP + n]

    pl.semaphore_wait(barrier, 3 + jnp.where(has_up, 1, 0) + jnp.where(has_down, 1, 0))

    sent = []

    def copy(h, t, b, f, to, sid):
        slot = buf.at[t, b, f, pl.ds(*ranges[h])]
        return pltpu.make_async_remote_copy(
            src_ref=slot, dst_ref=slot, send_sem=ssem.at[sid], recv_sem=rsem.at[h, t, b, f],
            device_id=to, device_id_type=MESH,
        )

    def send(h, t, b, f, to, cond=None):
        sid = len(sent)
        sent.append((h, t, b, f, to, cond))
        if cond is None:
            copy(h, t, b, f, to, sid).start()
        else:
            @pl.when(cond)
            def _():
                copy(h, t, b, f, to, sid).start()

    def wait_sent():
        for sid, (h, t, b, f, to, cond) in enumerate(sent):
            if cond is None:
                copy(h, t, b, f, to, sid).wait_send()
            else:
                @pl.when(cond)
                def _():
                    copy(h, t, b, f, to, sid).wait_send()

    def arrive(h, t, b, f):
        copy(h, t, b, f, (blk, feat_c), 0).wait_recv()

    def relay(h, t, i, dy, dx):
        order = orders[h][t]
        far = {"z": i, "y": dy, "x": dx}
        came = max([n for n, axis in enumerate(order) if far[axis]], default=-1)
        b, f = place(i, dy), feat_x if dx else feat
        if came >= 0:
            arrive(h, t, b, f)
        if i and order[came] == "z":
            send(h, t, b, f, (blk + 2, feat), jnp.logical_and(planes[i] < z, has_up))
            send(h, t, b, f, (blk - 2, feat), jnp.logical_and(planes[i] > z, has_down))
        for axis in order[came + 1:]:
            if axis == "z":
                send(h, t, b, f, (blk + 2, feat), has_up)
                send(h, t, b, f, (blk - 2, feat), has_down)
            else:
                send(h, t, b, f, (blk, feat_x) if axis == "x" else (blk_y, feat))
        send(h, t, b, f, (blk, feat_c), None if i == 0 and dy == 0 else c == t)

    scale, bias = scale_ref[0], bias_ref[0]

    def unpack(out, t, b):
        for q in range(groups):
            n = min(GROUP, rows - q * GROUP)
            for f in range(4):
                out[q * GROUP:q * GROUP + n, f * rem:(f + 1) * rem] = (
                    buf[t, b, f, rows:rows + n, q * rem:(q + 1) * rem])

    def hand(b):
        return pltpu.make_async_remote_copy(
            src_ref=slope_buf.at[c, b], dst_ref=slope_buf.at[c, b],
            send_sem=slope_ssem.at[b], recv_sem=slope_rsem.at[b],
            device_id=(blk, feat_c), device_id_type=MESH,
        )

    def finish(i, dy):
        b = place(i, dy)
        for h in (0, 1):
            for f in (feat_c, feat_xc):
                arrive(h, u, b, f)
                if i == 0 and dy == 0:
                    arrive(h, c, b, f)
        if i == 0 and dy == 0:
            unpack(mine, c, b)
        unpack(theirs, u, b)
        dots = dot_nt(mine[...], theirs[...])
        for f in range(4):
            dots += dot_nt(buf[c, blk, f, 0:rows, :], buf[u, b, f, 0:rows, :])
        logit = scale * dots + bias
        if i == 0 and dy == 0:
            diag = (lax.broadcasted_iota(jnp.int32, logit.shape, 0)
                    == lax.broadcasted_iota(jnp.int32, logit.shape, 1))
            value = jax.nn.sigmoid(jnp.where(diag, -logit, logit))
            value = jnp.where(diag, -value, value)
        else:
            value = jax.nn.sigmoid(logit)
        slope_buf[c, b] = value.astype(BF16)
        hand(b).start()

    def apply(i, dy):
        b = place(i, dy)
        for t in (0, 1):
            for q in range(groups):
                n = min(GROUP, rows - q * GROUP)
                own_rem[t, q * GROUP:q * GROUP + n, :] = (
                    buf[t, b, feat, rows:rows + n, q * rem:(q + 1) * rem])
        pltpu.make_async_remote_copy(
            src_ref=slope_buf.at[u, b], dst_ref=slope_buf.at[u, b],
            send_sem=slope_ssem.at[b], recv_sem=slope_rsem.at[b],
            device_id=(blk, feat_c), device_id_type=MESH,
        ).wait_recv()
        for t in (0, 1):
            slope = slope_buf[t, b]
            acc[t] += jnp.dot(slope, buf[1 - t, b, feat, 0:rows, :], preferred_element_type=F32)
            accr[t] += jnp.dot(slope, own_rem[1 - t], preferred_element_type=F32)

    acc[...] = jnp.zeros_like(acc)
    accr[...] = jnp.zeros_like(accr)

    def steps(codes):
        sent.clear()
        slopes = 0
        for step in codes:
            kind, part, i, dy, dx = step // 64, step // 16 % 4, step // 4 % 4, step // 2 % 2, step % 2
            if kind == 0:
                relay(part // 2, part % 2, i, dy, dx)
            elif kind == 1:
                finish(i, dy)
                slopes += 1
                if slopes == 2 * nz:
                    wait_sent()
            else:
                apply(i, dy)

    for inner, codes in enumerate(STEPS):
        @pl.when((near > 0) == bool(inner))
        def _():
            steps(codes)

    for t, ref in ((0, gi_ref), (1, gt_ref)):
        ref[:, 0:wide] = scale * acc[t]
        ref[:, wide:wide + rem] = scale * accr[t]
    for b in range(nz * 2):
        hand(b).wait_send()


def gathered(blocks, image, text, scale, bias):
    rows, width = image.shape
    wide = width // 128 * 128
    rem = width - wide
    nz = blocks // 2
    out = jax.ShapeDtypeStruct((rows, width), F32)
    return pl.pallas_call(
        functools.partial(kernel, nz, rows, wide, rem),
        out_shape=(out, out),
        in_specs=[pl.BlockSpec(memory_space=pl.ANY)] * 2
        + [pl.BlockSpec(memory_space=pltpu.SMEM)] * 2,
        out_specs=(pl.BlockSpec(memory_space=pltpu.VMEM),) * 2,
        scratch_shapes=[
            pltpu.VMEM((2, rows, width), BF16),
            pltpu.SemaphoreType.DMA((2,)),
            pltpu.VMEM((2, blocks, 4, rows + GROUP, wide), BF16),
            pltpu.VMEM((2, blocks, rows, rows), BF16),
            pltpu.VMEM((rows, 4 * rem), BF16),
            pltpu.VMEM((rows, 4 * rem), BF16),
            pltpu.VMEM((2, rows, rem), BF16),
            pltpu.VMEM((2, rows, wide), F32),
            pltpu.VMEM((2, rows, rem), F32),
            pltpu.SemaphoreType.DMA((44 * nz,)),
            pltpu.SemaphoreType.DMA((2, 2, blocks, 4)),
            pltpu.SemaphoreType.DMA((blocks,)),
            pltpu.SemaphoreType.DMA((blocks,)),
        ],
        compiler_params=pltpu.CompilerParams(
            collective_id=0, has_side_effects=True, vmem_limit_bytes=121 * 2**19
        ),
    )(image, text, scale.reshape(1), bias.reshape(1))


def solution(mesh):
    in_specs = (P("blk", "feat"), P("blk", "feat"), P(), P())
    out_specs = (P("blk", "feat"), P("blk", "feat"))
    blocks, feats = mesh.shape["blk"], mesh.shape["feat"]

    def body(image, text, scale, bias):
        whole = 2 * blocks * feats * image.size * 2
        if feats == 4 and blocks == 2 * PLANES and whole <= 16 * 2**20:
            return gathered(blocks, image, text, scale, bias)
        return shards(image, text, scale, bias)

    return jax.shard_map(body, mesh=mesh, in_specs=in_specs, out_specs=out_specs, check_vma=False)
```

```python
import functools
import jax
import jax.numpy as jnp
from jax import lax
from jax.experimental import pallas as pl
from jax.experimental.pallas import tpu as pltpu
from jax.sharding import PartitionSpec as P


def from_behind(block, axis, distance):
    devices = range(lax.axis_size(axis))
    route = [((i - distance) % len(devices), i) for i in devices]
    return lax.ppermute(block, axis, route)


def pair_grads(image_all, current, scale, bias, diag_start, own):
    dots = lax.dot_general(
        image_all, current, (((1,), (1,)), ((), ())), preferred_element_type=jnp.float32
    )
    logit = scale * dots + bias
    if own:
        row_index = lax.broadcasted_iota(jnp.int32, logit.shape, 0)
        col_index = diag_start + lax.broadcasted_iota(jnp.int32, logit.shape, 1)
        value = jnp.where(row_index == col_index, -jax.nn.sigmoid(-logit), jax.nn.sigmoid(logit))
    else:
        value = jax.nn.sigmoid(logit)
    slope = value.astype(jnp.bfloat16)
    image_add = jnp.dot(slope, current, preferred_element_type=jnp.float32)
    text_add = lax.dot_general(
        slope, image_all, (((0,), (0,)), ((), ())), preferred_element_type=jnp.float32
    )
    return (image_add, text_add)


def pass_both(current, accum):
    return (
        from_behind(current.astype(jnp.float32), "blk", 1).astype(current.dtype),
        from_behind(accum, "blk", 1),
    )


def shards(image, text, scale, bias):
    block_count = lax.axis_size("blk")
    image_all = lax.all_gather(image, "feat", axis=1, tiled=True)
    quarter = lax.all_to_all(text, "feat", split_axis=0, concat_axis=1, tiled=True)
    rows_q = quarter.shape[0]
    diag_start = lax.axis_index("feat") * rows_q
    image_acc, text_acc = pair_grads(image_all, quarter, scale, bias, diag_start, True)

    def visit(step, carry):
        current, accum, grad_img = carry
        current, accum = pass_both(current, accum)
        image_add, text_add = pair_grads(image_all, current, scale, bias, 0, False)
        return (current, accum + text_add, grad_img + image_add)

    current, text_acc, image_acc = lax.fori_loop(
        1, block_count, visit, (quarter, text_acc, image_acc)
    )
    text_acc = from_behind(text_acc, "blk", 1)
    image_grad = scale * lax.psum_scatter(image_acc, "feat", scatter_dimension=1, tiled=True)
    text_grad = lax.all_to_all(scale * text_acc, "feat", split_axis=1, concat_axis=0, tiled=True)
    return (image_grad, text_grad)


MESH = pl.DeviceIdType.MESH
BF16 = jnp.bfloat16
F32 = jnp.float32
STEPS = (
    (
        48, 0, 32, 49, 52, 2, 16, 34, 20, 1, 50, 4, 36, 18, 17, 51, 38, 35, 53, 8,
        33, 24, 40, 5, 6, 37, 19, 54, 21, 22, 56, 9, 10, 64, 42, 25, 28, 3, 23, 26,
        68, 58, 55, 41, 39, 12, 44, 7, 57, 66, 11, 43, 27, 60, 29, 132, 14, 46, 72, 59,
        61, 70, 45, 62, 130, 31, 30, 13, 15, 74, 47, 63, 128, 76, 78, 138, 134, 140, 136, 142,
    ),
    (
        48, 32, 0, 16, 49, 34, 8, 1, 36, 4, 17, 33, 24, 20, 52, 40, 56, 2, 6, 38,
        51, 18, 19, 42, 28, 35, 44, 64, 37, 21, 9, 12, 53, 50, 3, 57, 41, 128, 60, 25,
        10, 39, 46, 5, 14, 66, 61, 72, 22, 55, 26, 7, 54, 30, 23, 45, 58, 62, 29, 13,
        68, 11, 27, 43, 59, 130, 70, 31, 15, 47, 63, 132, 76, 74, 78, 134, 140, 136, 138, 142,
    ),
)
PLANES = 4
GROUP = 32


def round_up(value, unit):
    return -(-value // unit) * unit


def dot_nt(a, b):
    return lax.dot_general(a, b, (((1,), (1,)), ((), ())), preferred_element_type=F32)


def kernel(nz, rows, wide, rem, img_ref, txt_ref, scale_ref, bias_ref, gi_ref, gt_ref,
           own_in, in_sem, buf, slope_buf, mine, theirs, own_rem, acc, accr,
           ssem, rsem, slope_ssem, slope_rsem):
    blk, feat = lax.axis_index("blk"), lax.axis_index("feat")
    z, y = blk // 2, blk % 2
    x, c = feat // 2, feat % 2
    u = 1 - c
    blk_y = z * 2 + 1 - y
    feat_x = (1 - x) * 2 + c
    feat_c = x * 2 + 1 - c
    feat_xc = (1 - x) * 2 + 1 - c
    near = jnp.minimum(z, nz - 1 - z)
    groups = -(-rows // GROUP)
    cut = (rows + GROUP) * 5 // 13 // 16 * 16
    has_up, has_down = z < nz - 1, z > 0
    ranges = ((0, cut), (cut, rows + GROUP - cut))
    orders = (("zyx", "zxy"), ("yzx", "xzy"))

    def item(i):
        k = jnp.where(i <= 2 * near, (i + 1) // 2, i - near)
        below = jnp.where(i <= 2 * near, i % 2, jnp.where(z > near, 1, 0))
        return jnp.where(below == 1, z - k, z + k)

    planes = [z] + [item(i) for i in range(1, nz)]

    def along_z(act):
        @pl.when(has_up)
        def _():
            act((blk + 2, feat))

        @pl.when(has_down)
        def _():
            act((blk - 2, feat))

    def place(i, dy):
        return planes[i] * 2 + (1 - y if dy else y)

    loads = [pltpu.make_async_copy(ref, own_in.at[t], in_sem.at[t])
             for t, ref in enumerate((img_ref, txt_ref))]
    for load in loads:
        load.start()

    barrier = pltpu.get_barrier_semaphore()

    def greet(to):
        pl.semaphore_signal(barrier, inc=1, device_id=to, device_id_type=MESH)

    for to in ((blk_y, feat), (blk, feat_x), (blk, feat_c)):
        greet(to)
    along_z(greet)

    for t in (0, 1):
        loads[t].wait()
        buf[t, blk, feat, 0:rows, :] = own_in[t, :, 0:wide]
        last = own_in[t, :, wide:wide + rem]
        for q in range(groups):
            n = min(GROUP, rows - q * GROUP)
            buf[t, blk, feat, rows:rows + n, q * rem:(q + 1) * rem] = last[q * GROUP:q * GROUP + n]

    pl.semaphore_wait(barrier, 3 + jnp.where(has_up, 1, 0) + jnp.where(has_down, 1, 0))

    sent = []

    def copy(h, t, b, f, to, sid):
        slot = buf.at[t, b, f, pl.ds(*ranges[h])]
        return pltpu.make_async_remote_copy(
            src_ref=slot, dst_ref=slot, send_sem=ssem.at[sid], recv_sem=rsem.at[h, t, b, f],
            device_id=to, device_id_type=MESH,
        )

    def send(h, t, b, f, to, cond=None):
        sid = len(sent)
        sent.append((h, t, b, f, to, cond))
        if cond is None:
            copy(h, t, b, f, to, sid).start()
        else:
            @pl.when(cond)
            def _():
                copy(h, t, b, f, to, sid).start()

    def wait_sent():
        for sid, (h, t, b, f, to, cond) in enumerate(sent):
            if cond is None:
                copy(h, t, b, f, to, sid).wait_send()
            else:
                @pl.when(cond)
                def _():
                    copy(h, t, b, f, to, sid).wait_send()

    def arrive(h, t, b, f):
        copy(h, t, b, f, (blk, feat_c), 0).wait_recv()

    def relay(h, t, i, dy, dx):
        order = orders[h][t]
        far = {"z": i, "y": dy, "x": dx}
        came = max([n for n, axis in enumerate(order) if far[axis]], default=-1)
        b, f = place(i, dy), feat_x if dx else feat
        if came >= 0:
            arrive(h, t, b, f)
        if i and order[came] == "z":
            send(h, t, b, f, (blk + 2, feat), jnp.logical_and(planes[i] < z, has_up))
            send(h, t, b, f, (blk - 2, feat), jnp.logical_and(planes[i] > z, has_down))
        for axis in order[came + 1:]:
            if axis == "z":
                send(h, t, b, f, (blk + 2, feat), has_up)
                send(h, t, b, f, (blk - 2, feat), has_down)
            else:
                send(h, t, b, f, (blk, feat_x) if axis == "x" else (blk_y, feat))
        send(h, t, b, f, (blk, feat_c), None if i == 0 and dy == 0 else c == t)

    scale, bias = scale_ref[0], bias_ref[0]

    def unpack(out, t, b):
        for q in range(groups):
            n = min(GROUP, rows - q * GROUP)
            for f in range(4):
                out[q * GROUP:q * GROUP + n, f * rem:(f + 1) * rem] = (
                    buf[t, b, f, rows:rows + n, q * rem:(q + 1) * rem])

    def hand(b):
        return pltpu.make_async_remote_copy(
            src_ref=slope_buf.at[c, b], dst_ref=slope_buf.at[c, b],
            send_sem=slope_ssem.at[b], recv_sem=slope_rsem.at[b],
            device_id=(blk, feat_c), device_id_type=MESH,
        )

    def finish(i, dy):
        b = place(i, dy)
        for h in (0, 1):
            for f in (feat_c, feat_xc):
                arrive(h, u, b, f)
                if i == 0 and dy == 0:
                    arrive(h, c, b, f)
        if i == 0 and dy == 0:
            unpack(mine, c, b)
        unpack(theirs, u, b)
        dots = dot_nt(mine[...], theirs[...])
        for f in range(4):
            dots += dot_nt(buf[c, blk, f, 0:rows, :], buf[u, b, f, 0:rows, :])
        logit = scale * dots + bias
        if i == 0 and dy == 0:
            diag = (lax.broadcasted_iota(jnp.int32, logit.shape, 0)
                    == lax.broadcasted_iota(jnp.int32, logit.shape, 1))
            value = jax.nn.sigmoid(jnp.where(diag, -logit, logit))
            value = jnp.where(diag, -value, value)
        else:
            value = jax.nn.sigmoid(logit)
        slope_buf[c, b] = value.astype(BF16)
        hand(b).start()

    def apply(i, dy):
        b = place(i, dy)
        for t in (0, 1):
            for q in range(groups):
                n = min(GROUP, rows - q * GROUP)
                own_rem[t, q * GROUP:q * GROUP + n, :] = (
                    buf[t, b, feat, rows:rows + n, q * rem:(q + 1) * rem])
        pltpu.make_async_remote_copy(
            src_ref=slope_buf.at[u, b], dst_ref=slope_buf.at[u, b],
            send_sem=slope_ssem.at[b], recv_sem=slope_rsem.at[b],
            device_id=(blk, feat_c), device_id_type=MESH,
        ).wait_recv()
        for t in (0, 1):
            slope = slope_buf[t, b]
            acc[t] += jnp.dot(slope, buf[1 - t, b, feat, 0:rows, :], preferred_element_type=F32)
            accr[t] += jnp.dot(slope, own_rem[1 - t], preferred_element_type=F32)

    acc[...] = jnp.zeros_like(acc)
    accr[...] = jnp.zeros_like(accr)

    def steps(codes):
        sent.clear()
        slopes = 0
        for step in codes:
            kind, part, i, dy, dx = step // 64, step // 16 % 4, step // 4 % 4, step // 2 % 2, step % 2
            if kind == 0:
                relay(part // 2, part % 2, i, dy, dx)
            elif kind == 1:
                finish(i, dy)
                slopes += 1
                if slopes == 2 * nz:
                    wait_sent()
            else:
                apply(i, dy)

    for inner, codes in enumerate(STEPS):
        @pl.when((near > 0) == bool(inner))
        def _():
            steps(codes)

    for t, ref in ((0, gi_ref), (1, gt_ref)):
        ref[:, 0:wide] = scale * acc[t]
        ref[:, wide:wide + rem] = scale * accr[t]
    for b in range(nz * 2):
        hand(b).wait_send()


def gathered(blocks, image, text, scale, bias):
    rows, width = image.shape
    wide = width // 128 * 128
    rem = width - wide
    nz = blocks // 2
    out = jax.ShapeDtypeStruct((rows, width), F32)
    return pl.pallas_call(
        functools.partial(kernel, nz, rows, wide, rem),
        out_shape=(out, out),
        in_specs=[pl.BlockSpec(memory_space=pl.ANY)] * 2
        + [pl.BlockSpec(memory_space=pltpu.SMEM)] * 2,
        out_specs=(pl.BlockSpec(memory_space=pltpu.VMEM),) * 2,
        scratch_shapes=[
            pltpu.VMEM((2, rows, width), BF16),
            pltpu.SemaphoreType.DMA((2,)),
            pltpu.VMEM((2, blocks, 4, rows + GROUP, wide), BF16),
            pltpu.VMEM((2, blocks, rows, rows), BF16),
            pltpu.VMEM((rows, 4 * rem), BF16),
            pltpu.VMEM((rows, 4 * rem), BF16),
            pltpu.VMEM((2, rows, rem), BF16),
            pltpu.VMEM((2, rows, wide), F32),
            pltpu.VMEM((2, rows, rem), F32),
            pltpu.SemaphoreType.DMA((44 * nz,)),
            pltpu.SemaphoreType.DMA((2, 2, blocks, 4)),
            pltpu.SemaphoreType.DMA((blocks,)),
            pltpu.SemaphoreType.DMA((blocks,)),
        ],
        compiler_params=pltpu.CompilerParams(
            collective_id=0, has_side_effects=True, vmem_limit_bytes=60 * 2**20
        ),
    )(image, text, scale.reshape(1), bias.reshape(1))


def solution(mesh):
    in_specs = (P("blk", "feat"), P("blk", "feat"), P(), P())
    out_specs = (P("blk", "feat"), P("blk", "feat"))
    blocks, feats = mesh.shape["blk"], mesh.shape["feat"]

    def body(image, text, scale, bias):
        whole = 2 * blocks * feats * image.size * 2
        if feats == 4 and blocks == 2 * PLANES and whole <= 16 * 2**20:
            return gathered(blocks, image, text, scale, bias)
        return shards(image, text, scale, bias)

    return jax.shard_map(body, mesh=mesh, in_specs=in_specs, out_specs=out_specs, check_vma=False)
```

```python
import functools
import jax
import jax.numpy as jnp
from jax import lax
from jax.experimental import pallas as pl
from jax.experimental.pallas import tpu as pltpu
from jax.sharding import PartitionSpec as P


def from_behind(block, axis, distance):
    devices = range(lax.axis_size(axis))
    route = [((i - distance) % len(devices), i) for i in devices]
    return lax.ppermute(block, axis, route)


def pair_grads(image_all, current, scale, bias, diag_start, own):
    dots = lax.dot_general(
        image_all, current, (((1,), (1,)), ((), ())), preferred_element_type=jnp.float32
    )
    logit = scale * dots + bias
    if own:
        row_index = lax.broadcasted_iota(jnp.int32, logit.shape, 0)
        col_index = diag_start + lax.broadcasted_iota(jnp.int32, logit.shape, 1)
        value = jnp.where(row_index == col_index, -jax.nn.sigmoid(-logit), jax.nn.sigmoid(logit))
    else:
        value = jax.nn.sigmoid(logit)
    slope = value.astype(jnp.bfloat16)
    image_add = jnp.dot(slope, current, preferred_element_type=jnp.float32)
    text_add = lax.dot_general(
        slope, image_all, (((0,), (0,)), ((), ())), preferred_element_type=jnp.float32
    )
    return (image_add, text_add)


def pass_both(current, accum):
    return (
        from_behind(current.astype(jnp.float32), "blk", 1).astype(current.dtype),
        from_behind(accum, "blk", 1),
    )


def shards(image, text, scale, bias):
    block_count = lax.axis_size("blk")
    image_all = lax.all_gather(image, "feat", axis=1, tiled=True)
    quarter = lax.all_to_all(text, "feat", split_axis=0, concat_axis=1, tiled=True)
    rows_q = quarter.shape[0]
    diag_start = lax.axis_index("feat") * rows_q
    image_acc, text_acc = pair_grads(image_all, quarter, scale, bias, diag_start, True)

    def visit(step, carry):
        current, accum, grad_img = carry
        current, accum = pass_both(current, accum)
        image_add, text_add = pair_grads(image_all, current, scale, bias, 0, False)
        return (current, accum + text_add, grad_img + image_add)

    current, text_acc, image_acc = lax.fori_loop(
        1, block_count, visit, (quarter, text_acc, image_acc)
    )
    text_acc = from_behind(text_acc, "blk", 1)
    image_grad = scale * lax.psum_scatter(image_acc, "feat", scatter_dimension=1, tiled=True)
    text_grad = lax.all_to_all(scale * text_acc, "feat", split_axis=1, concat_axis=0, tiled=True)
    return (image_grad, text_grad)


MESH = pl.DeviceIdType.MESH
BF16 = jnp.bfloat16
F32 = jnp.float32
STEPS = (
    (
        48, 0, 32, 16, 2, 36, 49, 4, 34, 52, 20, 50, 18, 1, 38, 17, 8, 3, 53, 33,
        5, 37, 54, 51, 24, 35, 21, 6, 40, 22, 10, 39, 56, 64, 42, 9, 25, 55, 19, 68,
        28, 26, 58, 41, 23, 12, 11, 27, 44, 57, 7, 66, 43, 60, 14, 13, 29, 72, 46, 59,
        61, 70, 130, 31, 45, 15, 74, 30, 63, 62, 47, 128, 134, 76, 78, 138, 132, 136, 140, 142,
    ),
    (
        48, 32, 0, 16, 49, 33, 34, 1, 4, 8, 36, 17, 20, 24, 2, 40, 52, 18, 56, 6,
        50, 38, 35, 42, 37, 28, 12, 64, 44, 57, 53, 9, 51, 41, 19, 21, 3, 7, 60, 25,
        5, 10, 128, 39, 46, 61, 66, 23, 14, 29, 55, 72, 58, 54, 45, 22, 11, 62, 68, 27,
        59, 43, 26, 30, 47, 13, 70, 15, 130, 31, 63, 74, 76, 78, 134, 136, 132, 138, 140, 142,
    ),
)
PLANES = 4
GROUP = 32


def round_up(value, unit):
    return -(-value // unit) * unit


def dot_nt(a, b):
    return lax.dot_general(a, b, (((1,), (1,)), ((), ())), preferred_element_type=F32)


def kernel(nz, rows, wide, rem, img_ref, txt_ref, scale_ref, bias_ref, gi_ref, gt_ref,
           own_in, in_sem, buf, slope_buf, mine, theirs, own_rem, acc, accr,
           ssem, rsem, slope_ssem, slope_rsem):
    blk, feat = lax.axis_index("blk"), lax.axis_index("feat")
    z, y = blk // 2, blk % 2
    x, c = feat // 2, feat % 2
    u = 1 - c
    blk_y = z * 2 + 1 - y
    feat_x = (1 - x) * 2 + c
    feat_c = x * 2 + 1 - c
    feat_xc = (1 - x) * 2 + 1 - c
    near = jnp.minimum(z, nz - 1 - z)
    groups = -(-rows // GROUP)
    cut = (rows + GROUP) * 5 // 13 // 16 * 16
    has_up, has_down = z < nz - 1, z > 0
    ranges = ((0, cut), (cut, rows + GROUP - cut))
    orders = (("zyx", "zxy"), ("yzx", "xzy"))

    def item(i):
        k = jnp.where(i <= 2 * near, (i + 1) // 2, i - near)
        below = jnp.where(i <= 2 * near, i % 2, jnp.where(z > near, 1, 0))
        return jnp.where(below == 1, z - k, z + k)

    planes = [z] + [item(i) for i in range(1, nz)]

    def along_z(act):
        @pl.when(has_up)
        def _():
            act((blk + 2, feat))

        @pl.when(has_down)
        def _():
            act((blk - 2, feat))

    def place(i, dy):
        return planes[i] * 2 + (1 - y if dy else y)

    loads = [pltpu.make_async_copy(ref, own_in.at[t], in_sem.at[t])
             for t, ref in enumerate((img_ref, txt_ref))]
    for load in loads:
        load.start()

    barrier = pltpu.get_barrier_semaphore()

    def greet(to):
        pl.semaphore_signal(barrier, inc=1, device_id=to, device_id_type=MESH)

    for to in ((blk_y, feat), (blk, feat_x), (blk, feat_c)):
        greet(to)
    along_z(greet)

    for t in (0, 1):
        loads[t].wait()
        buf[t, blk, feat, 0:rows, :] = own_in[t, :, 0:wide]
        last = own_in[t, :, wide:wide + rem]
        for q in range(groups):
            n = min(GROUP, rows - q * GROUP)
            buf[t, blk, feat, rows:rows + n, q * rem:(q + 1) * rem] = last[q * GROUP:q * GROUP + n]

    pl.semaphore_wait(barrier, 3 + jnp.where(has_up, 1, 0) + jnp.where(has_down, 1, 0))

    sent = []

    def copy(h, t, b, f, to, sid):
        slot = buf.at[t, b, f, pl.ds(*ranges[h])]
        return pltpu.make_async_remote_copy(
            src_ref=slot, dst_ref=slot, send_sem=ssem.at[sid], recv_sem=rsem.at[h, t, b, f],
            device_id=to, device_id_type=MESH,
        )

    def send(h, t, b, f, to, cond=None):
        sid = len(sent)
        sent.append((h, t, b, f, to, cond))
        if cond is None:
            copy(h, t, b, f, to, sid).start()
        else:
            @pl.when(cond)
            def _():
                copy(h, t, b, f, to, sid).start()

    def wait_sent():
        for sid, (h, t, b, f, to, cond) in enumerate(sent):
            if cond is None:
                copy(h, t, b, f, to, sid).wait_send()
            else:
                @pl.when(cond)
                def _():
                    copy(h, t, b, f, to, sid).wait_send()

    def arrive(h, t, b, f):
        copy(h, t, b, f, (blk, feat_c), 0).wait_recv()

    def relay(h, t, i, dy, dx):
        order = orders[h][t]
        far = {"z": i, "y": dy, "x": dx}
        came = max([n for n, axis in enumerate(order) if far[axis]], default=-1)
        b, f = place(i, dy), feat_x if dx else feat
        if came >= 0:
            arrive(h, t, b, f)
        if i and order[came] == "z":
            send(h, t, b, f, (blk + 2, feat), jnp.logical_and(planes[i] < z, has_up))
            send(h, t, b, f, (blk - 2, feat), jnp.logical_and(planes[i] > z, has_down))
        for axis in order[came + 1:]:
            if axis == "z":
                send(h, t, b, f, (blk + 2, feat), has_up)
                send(h, t, b, f, (blk - 2, feat), has_down)
            else:
                send(h, t, b, f, (blk, feat_x) if axis == "x" else (blk_y, feat))
        send(h, t, b, f, (blk, feat_c), None if i == 0 and dy == 0 else c == t)

    scale, bias = scale_ref[0], bias_ref[0]

    def unpack(out, t, b):
        for q in range(groups):
            n = min(GROUP, rows - q * GROUP)
            for f in range(4):
                out[q * GROUP:q * GROUP + n, f * rem:(f + 1) * rem] = (
                    buf[t, b, f, rows:rows + n, q * rem:(q + 1) * rem])

    def hand(b):
        return pltpu.make_async_remote_copy(
            src_ref=slope_buf.at[c, b], dst_ref=slope_buf.at[c, b],
            send_sem=slope_ssem.at[b], recv_sem=slope_rsem.at[b],
            device_id=(blk, feat_c), device_id_type=MESH,
        )

    def finish(i, dy):
        b = place(i, dy)
        for h in (0, 1):
            for f in (feat_c, feat_xc):
                arrive(h, u, b, f)
                if i == 0 and dy == 0:
                    arrive(h, c, b, f)
        if i == 0 and dy == 0:
            unpack(mine, c, b)
        unpack(theirs, u, b)
        dots = dot_nt(mine[...], theirs[...])
        for f in range(4):
            dots += dot_nt(buf[c, blk, f, 0:rows, :], buf[u, b, f, 0:rows, :])
        logit = scale * dots + bias
        if i == 0 and dy == 0:
            diag = (lax.broadcasted_iota(jnp.int32, logit.shape, 0)
                    == lax.broadcasted_iota(jnp.int32, logit.shape, 1))
            value = jax.nn.sigmoid(jnp.where(diag, -logit, logit))
            value = jnp.where(diag, -value, value)
        else:
            value = jax.nn.sigmoid(logit)
        slope_buf[c, b] = value.astype(BF16)
        hand(b).start()

    def apply(i, dy):
        b = place(i, dy)
        for t in (0, 1):
            for q in range(groups):
                n = min(GROUP, rows - q * GROUP)
                own_rem[t, q * GROUP:q * GROUP + n, :] = (
                    buf[t, b, feat, rows:rows + n, q * rem:(q + 1) * rem])
        pltpu.make_async_remote_copy(
            src_ref=slope_buf.at[u, b], dst_ref=slope_buf.at[u, b],
            send_sem=slope_ssem.at[b], recv_sem=slope_rsem.at[b],
            device_id=(blk, feat_c), device_id_type=MESH,
        ).wait_recv()
        for t in (0, 1):
            slope = slope_buf[t, b]
            acc[t] += jnp.dot(slope, buf[1 - t, b, feat, 0:rows, :], preferred_element_type=F32)
            accr[t] += jnp.dot(slope, own_rem[1 - t], preferred_element_type=F32)

    acc[...] = jnp.zeros_like(acc)
    accr[...] = jnp.zeros_like(accr)

    def steps(codes):
        sent.clear()
        slopes = 0
        for step in codes:
            kind, part, i, dy, dx = step // 64, step // 16 % 4, step // 4 % 4, step // 2 % 2, step % 2
            if kind == 0:
                relay(part // 2, part % 2, i, dy, dx)
            elif kind == 1:
                finish(i, dy)
                slopes += 1
                if slopes == 2 * nz:
                    wait_sent()
            else:
                apply(i, dy)

    for inner, codes in enumerate(STEPS):
        @pl.when((near > 0) == bool(inner))
        def _():
            steps(codes)

    for t, ref in ((0, gi_ref), (1, gt_ref)):
        ref[:, 0:wide] = scale * acc[t]
        ref[:, wide:wide + rem] = scale * accr[t]
    for b in range(nz * 2):
        hand(b).wait_send()


def gathered(blocks, image, text, scale, bias):
    rows, width = image.shape
    wide = width // 128 * 128
    rem = width - wide
    nz = blocks // 2
    out = jax.ShapeDtypeStruct((rows, width), F32)
    return pl.pallas_call(
        functools.partial(kernel, nz, rows, wide, rem),
        out_shape=(out, out),
        in_specs=[pl.BlockSpec(memory_space=pl.ANY)] * 2
        + [pl.BlockSpec(memory_space=pltpu.SMEM)] * 2,
        out_specs=(pl.BlockSpec(memory_space=pltpu.VMEM),) * 2,
        scratch_shapes=[
            pltpu.VMEM((2, rows, width), BF16),
            pltpu.SemaphoreType.DMA((2,)),
            pltpu.VMEM((2, blocks, 4, rows + GROUP, wide), BF16),
            pltpu.VMEM((2, blocks, rows, rows), BF16),
            pltpu.VMEM((rows, 4 * rem), BF16),
            pltpu.VMEM((rows, 4 * rem), BF16),
            pltpu.VMEM((2, rows, rem), BF16),
            pltpu.VMEM((2, rows, wide), F32),
            pltpu.VMEM((2, rows, rem), F32),
            pltpu.SemaphoreType.DMA((44 * nz,)),
            pltpu.SemaphoreType.DMA((2, 2, blocks, 4)),
            pltpu.SemaphoreType.DMA((blocks,)),
            pltpu.SemaphoreType.DMA((blocks,)),
        ],
        compiler_params=pltpu.CompilerParams(
            collective_id=0, has_side_effects=True, vmem_limit_bytes=60 * 2**20
        ),
    )(image, text, scale.reshape(1), bias.reshape(1))


def solution(mesh):
    in_specs = (P("blk", "feat"), P("blk", "feat"), P(), P())
    out_specs = (P("blk", "feat"), P("blk", "feat"))
    blocks, feats = mesh.shape["blk"], mesh.shape["feat"]

    def body(image, text, scale, bias):
        whole = 2 * blocks * feats * image.size * 2
        if feats == 4 and blocks == 2 * PLANES and whole <= 16 * 2**20:
            return gathered(blocks, image, text, scale, bias)
        return shards(image, text, scale, bias)

    return jax.shard_map(body, mesh=mesh, in_specs=in_specs, out_specs=out_specs, check_vma=False)
```

```python
import functools
import jax
import jax.numpy as jnp
from jax import lax
from jax.experimental import pallas as pl
from jax.experimental.pallas import tpu as pltpu
from jax.sharding import PartitionSpec as P


def from_behind(block, axis, distance):
    devices = range(lax.axis_size(axis))
    route = [((i - distance) % len(devices), i) for i in devices]
    return lax.ppermute(block, axis, route)


def pair_grads(image_all, current, scale, bias, diag_start, own):
    dots = lax.dot_general(
        image_all, current, (((1,), (1,)), ((), ())), preferred_element_type=jnp.float32
    )
    logit = scale * dots + bias
    if own:
        row_index = lax.broadcasted_iota(jnp.int32, logit.shape, 0)
        col_index = diag_start + lax.broadcasted_iota(jnp.int32, logit.shape, 1)
        value = jnp.where(row_index == col_index, -jax.nn.sigmoid(-logit), jax.nn.sigmoid(logit))
    else:
        value = jax.nn.sigmoid(logit)
    slope = value.astype(jnp.bfloat16)
    image_add = jnp.dot(slope, current, preferred_element_type=jnp.float32)
    text_add = lax.dot_general(
        slope, image_all, (((0,), (0,)), ((), ())), preferred_element_type=jnp.float32
    )
    return (image_add, text_add)


def pass_both(current, accum):
    return (
        from_behind(current.astype(jnp.float32), "blk", 1).astype(current.dtype),
        from_behind(accum, "blk", 1),
    )


def shards(image, text, scale, bias):
    block_count = lax.axis_size("blk")
    image_all = lax.all_gather(image, "feat", axis=1, tiled=True)
    quarter = lax.all_to_all(text, "feat", split_axis=0, concat_axis=1, tiled=True)
    rows_q = quarter.shape[0]
    diag_start = lax.axis_index("feat") * rows_q
    image_acc, text_acc = pair_grads(image_all, quarter, scale, bias, diag_start, True)

    def visit(step, carry):
        current, accum, grad_img = carry
        current, accum = pass_both(current, accum)
        image_add, text_add = pair_grads(image_all, current, scale, bias, 0, False)
        return (current, accum + text_add, grad_img + image_add)

    current, text_acc, image_acc = lax.fori_loop(
        1, block_count, visit, (quarter, text_acc, image_acc)
    )
    text_acc = from_behind(text_acc, "blk", 1)
    image_grad = scale * lax.psum_scatter(image_acc, "feat", scatter_dimension=1, tiled=True)
    text_grad = lax.all_to_all(scale * text_acc, "feat", split_axis=1, concat_axis=0, tiled=True)
    return (image_grad, text_grad)


MESH = pl.DeviceIdType.MESH
BF16 = jnp.bfloat16
F32 = jnp.float32
STEPS = (
    (
        48, 0, 32, 49, 52, 2, 16, 34, 20, 1, 50, 4, 36, 18, 17, 51, 38, 35, 53, 8,
        33, 24, 40, 5, 6, 37, 19, 54, 21, 22, 56, 9, 10, 64, 42, 25, 28, 3, 23, 26,
        68, 58, 55, 41, 39, 12, 44, 7, 57, 66, 11, 43, 27, 60, 29, 132, 14, 46, 72, 59,
        61, 70, 45, 62, 130, 31, 30, 13, 15, 74, 47, 63, 128, 76, 78, 138, 134, 140, 136, 142,
    ),
    (
        48, 32, 0, 16, 49, 34, 8, 1, 36, 4, 17, 33, 24, 20, 52, 40, 56, 2, 6, 38,
        51, 18, 19, 42, 28, 35, 44, 64, 37, 21, 9, 12, 53, 50, 3, 57, 41, 128, 60, 25,
        10, 39, 46, 5, 14, 66, 61, 72, 22, 55, 26, 7, 54, 30, 23, 45, 58, 62, 29, 13,
        68, 11, 27, 43, 59, 130, 70, 31, 15, 47, 63, 132, 76, 74, 78, 134, 140, 136, 138, 142,
    ),
)
PLANES = 4
GROUP = 32


def round_up(value, unit):
    return -(-value // unit) * unit


def dot_nt(a, b):
    return lax.dot_general(a, b, (((1,), (1,)), ((), ())), preferred_element_type=F32)


def kernel(nz, rows, wide, rem, img_ref, txt_ref, scale_ref, bias_ref, gi_ref, gt_ref,
           own_in, in_sem, buf, slope_buf, mine, theirs, own_rem, acc, accr,
           ssem, rsem, slope_ssem, slope_rsem):
    blk, feat = lax.axis_index("blk"), lax.axis_index("feat")
    z, y = blk // 2, blk % 2
    x, c = feat // 2, feat % 2
    u = 1 - c
    blk_y = z * 2 + 1 - y
    feat_x = (1 - x) * 2 + c
    feat_c = x * 2 + 1 - c
    feat_xc = (1 - x) * 2 + 1 - c
    near = jnp.minimum(z, nz - 1 - z)
    groups = -(-rows // GROUP)
    cut = (rows + GROUP) * 5 // 13 // 16 * 16
    has_up, has_down = z < nz - 1, z > 0
    ranges = ((0, cut), (cut, rows + GROUP - cut))
    orders = (("zyx", "zxy"), ("yzx", "xzy"))

    def item(i):
        k = jnp.where(i <= 2 * near, (i + 1) // 2, i - near)
        below = jnp.where(i <= 2 * near, i % 2, jnp.where(z > near, 1, 0))
        return jnp.where(below == 1, z - k, z + k)

    planes = [z] + [item(i) for i in range(1, nz)]

    def along_z(act):
        @pl.when(has_up)
        def _():
            act((blk + 2, feat))

        @pl.when(has_down)
        def _():
            act((blk - 2, feat))

    def place(i, dy):
        return planes[i] * 2 + (1 - y if dy else y)

    loads = [pltpu.make_async_copy(ref, own_in.at[t], in_sem.at[t])
             for t, ref in enumerate((img_ref, txt_ref))]
    for load in loads:
        load.start()

    barrier = pltpu.get_barrier_semaphore()

    def greet(to):
        pl.semaphore_signal(barrier, inc=1, device_id=to, device_id_type=MESH)

    for to in ((blk_y, feat), (blk, feat_x), (blk, feat_c)):
        greet(to)
    along_z(greet)

    for t in (0, 1):
        loads[t].wait()
        buf[t, blk, feat, 0:rows, :] = own_in[t, :, 0:wide]
        last = own_in[t, :, wide:wide + rem]
        for q in range(groups):
            n = min(GROUP, rows - q * GROUP)
            buf[t, blk, feat, rows:rows + n, q * rem:(q + 1) * rem] = last[q * GROUP:q * GROUP + n]

    pl.semaphore_wait(barrier, 3 + jnp.where(has_up, 1, 0) + jnp.where(has_down, 1, 0))

    sent = []

    def copy(h, t, b, f, to, sid):
        slot = buf.at[t, b, f, pl.ds(*ranges[h])]
        return pltpu.make_async_remote_copy(
            src_ref=slot, dst_ref=slot, send_sem=ssem.at[sid], recv_sem=rsem.at[h, t, b, f],
            device_id=to, device_id_type=MESH,
        )

    def send(h, t, b, f, to, cond=None):
        sid = len(sent)
        sent.append((h, t, b, f, to, cond))
        if cond is None:
            copy(h, t, b, f, to, sid).start()
        else:
            @pl.when(cond)
            def _():
                copy(h, t, b, f, to, sid).start()

    def wait_sent():
        for sid, (h, t, b, f, to, cond) in enumerate(sent):
            if cond is None:
                copy(h, t, b, f, to, sid).wait_send()
            else:
                @pl.when(cond)
                def _():
                    copy(h, t, b, f, to, sid).wait_send()

    def arrive(h, t, b, f):
        copy(h, t, b, f, (blk, feat_c), 0).wait_recv()

    def relay(h, t, i, dy, dx):
        order = orders[h][t]
        far = {"z": i, "y": dy, "x": dx}
        came = max([n for n, axis in enumerate(order) if far[axis]], default=-1)
        b, f = place(i, dy), feat_x if dx else feat
        if came >= 0:
            arrive(h, t, b, f)
        if i and order[came] == "z":
            send(h, t, b, f, (blk + 2, feat), jnp.logical_and(planes[i] < z, has_up))
            send(h, t, b, f, (blk - 2, feat), jnp.logical_and(planes[i] > z, has_down))
        for axis in order[came + 1:]:
            if axis == "z":
                send(h, t, b, f, (blk + 2, feat), has_up)
                send(h, t, b, f, (blk - 2, feat), has_down)
            else:
                send(h, t, b, f, (blk, feat_x) if axis == "x" else (blk_y, feat))
        send(h, t, b, f, (blk, feat_c), None if i == 0 and dy == 0 else c == t)

    scale, bias = scale_ref[0], bias_ref[0]

    def unpack(out, t, b):
        for q in range(groups):
            n = min(GROUP, rows - q * GROUP)
            for f in range(4):
                out[q * GROUP:q * GROUP + n, f * rem:(f + 1) * rem] = (
                    buf[t, b, f, rows:rows + n, q * rem:(q + 1) * rem])

    def hand(b):
        return pltpu.make_async_remote_copy(
            src_ref=slope_buf.at[c, b], dst_ref=slope_buf.at[c, b],
            send_sem=slope_ssem.at[b], recv_sem=slope_rsem.at[b],
            device_id=(blk, feat_c), device_id_type=MESH,
        )

    def finish(i, dy):
        b = place(i, dy)
        for h in (0, 1):
            for f in (feat_c, feat_xc):
                arrive(h, u, b, f)
                if i == 0 and dy == 0:
                    arrive(h, c, b, f)
        if i == 0 and dy == 0:
            unpack(mine, c, b)
        unpack(theirs, u, b)
        dots = dot_nt(mine[...], theirs[...])
        for f in range(4):
            dots += dot_nt(buf[c, blk, f, 0:rows, :], buf[u, b, f, 0:rows, :])
        logit = scale * dots + bias
        if i == 0 and dy == 0:
            diag = (lax.broadcasted_iota(jnp.int32, logit.shape, 0)
                    == lax.broadcasted_iota(jnp.int32, logit.shape, 1))
            value = jax.nn.sigmoid(jnp.where(diag, -logit, logit))
            value = jnp.where(diag, -value, value)
        else:
            value = jax.nn.sigmoid(logit)
        slope_buf[c, b] = value.astype(BF16)
        hand(b).start()

    def apply(i, dy):
        b = place(i, dy)
        for t in (0, 1):
            for q in range(groups):
                n = min(GROUP, rows - q * GROUP)
                own_rem[t, q * GROUP:q * GROUP + n, :] = (
                    buf[t, b, feat, rows:rows + n, q * rem:(q + 1) * rem])
        pltpu.make_async_remote_copy(
            src_ref=slope_buf.at[u, b], dst_ref=slope_buf.at[u, b],
            send_sem=slope_ssem.at[b], recv_sem=slope_rsem.at[b],
            device_id=(blk, feat_c), device_id_type=MESH,
        ).wait_recv()
        for t in (0, 1):
            slope = slope_buf[t, b]
            acc[t] += jnp.dot(slope, buf[1 - t, b, feat, 0:rows, :], preferred_element_type=F32)
            accr[t] += jnp.dot(slope, own_rem[1 - t], preferred_element_type=F32)

    acc[...] = jnp.zeros_like(acc)
    accr[...] = jnp.zeros_like(accr)

    def steps(codes):
        sent.clear()
        slopes = 0
        for step in codes:
            kind, part, i, dy, dx = step // 64, step // 16 % 4, step // 4 % 4, step // 2 % 2, step % 2
            if kind == 0:
                relay(part // 2, part % 2, i, dy, dx)
            elif kind == 1:
                finish(i, dy)
                slopes += 1
                if slopes == 2 * nz:
                    wait_sent()
            else:
                apply(i, dy)

    for inner, codes in enumerate(STEPS):
        @pl.when((near > 0) == bool(inner))
        def _():
            steps(codes)

    for t, ref in ((0, gi_ref), (1, gt_ref)):
        ref[:, 0:wide] = acc[t]
        ref[:, wide:wide + rem] = accr[t]
    for b in range(nz * 2):
        hand(b).wait_send()


def gathered(blocks, image, text, scale, bias):
    rows, width = image.shape
    wide = width // 128 * 128
    rem = width - wide
    nz = blocks // 2
    out = jax.ShapeDtypeStruct((rows, width), F32)
    image_sum, text_sum = pl.pallas_call(
        functools.partial(kernel, nz, rows, wide, rem),
        out_shape=(out, out),
        in_specs=[pl.BlockSpec(memory_space=pl.ANY)] * 2
        + [pl.BlockSpec(memory_space=pltpu.SMEM)] * 2,
        out_specs=(pl.BlockSpec(memory_space=pltpu.VMEM),) * 2,
        scratch_shapes=[
            pltpu.VMEM((2, rows, width), BF16),
            pltpu.SemaphoreType.DMA((2,)),
            pltpu.VMEM((2, blocks, 4, rows + GROUP, wide), BF16),
            pltpu.VMEM((2, blocks, rows, rows), BF16),
            pltpu.VMEM((rows, 4 * rem), BF16),
            pltpu.VMEM((rows, 4 * rem), BF16),
            pltpu.VMEM((2, rows, rem), BF16),
            pltpu.VMEM((2, rows, wide), F32),
            pltpu.VMEM((2, rows, rem), F32),
            pltpu.SemaphoreType.DMA((44 * nz,)),
            pltpu.SemaphoreType.DMA((2, 2, blocks, 4)),
            pltpu.SemaphoreType.DMA((blocks,)),
            pltpu.SemaphoreType.DMA((blocks,)),
        ],
        compiler_params=pltpu.CompilerParams(
            collective_id=0, has_side_effects=True, vmem_limit_bytes=60 * 2**20
        ),
    )(image, text, scale.reshape(1), bias.reshape(1))
    return scale * image_sum, scale * text_sum


def solution(mesh):
    in_specs = (P("blk", "feat"), P("blk", "feat"), P(), P())
    out_specs = (P("blk", "feat"), P("blk", "feat"))
    blocks, feats = mesh.shape["blk"], mesh.shape["feat"]

    def body(image, text, scale, bias):
        whole = 2 * blocks * feats * image.size * 2
        if feats == 4 and blocks == 2 * PLANES and whole <= 16 * 2**20:
            return gathered(blocks, image, text, scale, bias)
        return shards(image, text, scale, bias)

    return jax.shard_map(body, mesh=mesh, in_specs=in_specs, out_specs=out_specs, check_vma=False)
```

```python
import functools
import jax
import jax.numpy as jnp
from jax import lax
from jax.experimental import pallas as pl
from jax.experimental.pallas import tpu as pltpu
from jax.sharding import PartitionSpec as P


def from_behind(block, axis, distance):
    devices = range(lax.axis_size(axis))
    route = [((i - distance) % len(devices), i) for i in devices]
    return lax.ppermute(block, axis, route)


def pair_grads(image_all, current, scale, bias, diag_start, own):
    dots = lax.dot_general(
        image_all, current, (((1,), (1,)), ((), ())), preferred_element_type=jnp.float32
    )
    logit = scale * dots + bias
    if own:
        row_index = lax.broadcasted_iota(jnp.int32, logit.shape, 0)
        col_index = diag_start + lax.broadcasted_iota(jnp.int32, logit.shape, 1)
        value = jnp.where(row_index == col_index, -jax.nn.sigmoid(-logit), jax.nn.sigmoid(logit))
    else:
        value = jax.nn.sigmoid(logit)
    slope = value.astype(jnp.bfloat16)
    image_add = jnp.dot(slope, current, preferred_element_type=jnp.float32)
    text_add = lax.dot_general(
        slope, image_all, (((0,), (0,)), ((), ())), preferred_element_type=jnp.float32
    )
    return (image_add, text_add)


def pass_both(current, accum):
    return (
        from_behind(current.astype(jnp.float32), "blk", 1).astype(current.dtype),
        from_behind(accum, "blk", 1),
    )


def shards(image, text, scale, bias):
    block_count = lax.axis_size("blk")
    image_all = lax.all_gather(image, "feat", axis=1, tiled=True)
    quarter = lax.all_to_all(text, "feat", split_axis=0, concat_axis=1, tiled=True)
    rows_q = quarter.shape[0]
    diag_start = lax.axis_index("feat") * rows_q
    image_acc, text_acc = pair_grads(image_all, quarter, scale, bias, diag_start, True)

    def visit(step, carry):
        current, accum, grad_img = carry
        current, accum = pass_both(current, accum)
        image_add, text_add = pair_grads(image_all, current, scale, bias, 0, False)
        return (current, accum + text_add, grad_img + image_add)

    current, text_acc, image_acc = lax.fori_loop(
        1, block_count, visit, (quarter, text_acc, image_acc)
    )
    text_acc = from_behind(text_acc, "blk", 1)
    image_grad = scale * lax.psum_scatter(image_acc, "feat", scatter_dimension=1, tiled=True)
    text_grad = lax.all_to_all(scale * text_acc, "feat", split_axis=1, concat_axis=0, tiled=True)
    return (image_grad, text_grad)


MESH = pl.DeviceIdType.MESH
BF16 = jnp.bfloat16
F32 = jnp.float32
STEPS = (
    (
        48, 0, 32, 49, 52, 2, 16, 34, 20, 1, 50, 4, 36, 18, 17, 51, 38, 35, 53, 8,
        33, 24, 40, 5, 6, 37, 19, 54, 21, 22, 56, 9, 10, 64, 42, 25, 28, 3, 23, 26,
        68, 58, 55, 41, 39, 12, 44, 7, 57, 66, 11, 43, 27, 60, 29, 132, 14, 46, 72, 59,
        61, 70, 45, 62, 130, 31, 30, 13, 15, 74, 47, 63, 128, 76, 78, 138, 134, 140, 136, 142,
    ),
    (
        48, 32, 0, 16, 49, 33, 34, 1, 4, 8, 36, 17, 20, 24, 2, 40, 52, 18, 56, 6,
        50, 38, 35, 42, 37, 28, 12, 64, 44, 57, 53, 9, 51, 41, 19, 21, 3, 7, 60, 25,
        5, 10, 128, 39, 46, 61, 66, 23, 14, 29, 55, 72, 58, 54, 45, 22, 11, 62, 68, 27,
        59, 43, 26, 30, 47, 13, 70, 15, 130, 31, 63, 74, 76, 78, 134, 136, 132, 138, 140, 142,
    ),
)
PLANES = 4
GROUP = 32


def round_up(value, unit):
    return -(-value // unit) * unit


def dot_nt(a, b):
    return lax.dot_general(a, b, (((1,), (1,)), ((), ())), preferred_element_type=F32)


def kernel(nz, rows, wide, rem, img_ref, txt_ref, scale_ref, bias_ref, gi_ref, gt_ref,
           own_in, in_sem, buf, slope_buf, mine, theirs, own_rem, acc, accr,
           ssem, rsem, slope_ssem, slope_rsem):
    blk, feat = lax.axis_index("blk"), lax.axis_index("feat")
    z, y = blk // 2, blk % 2
    x, c = feat // 2, feat % 2
    u = 1 - c
    blk_y = z * 2 + 1 - y
    feat_x = (1 - x) * 2 + c
    feat_c = x * 2 + 1 - c
    feat_xc = (1 - x) * 2 + 1 - c
    near = jnp.minimum(z, nz - 1 - z)
    groups = -(-rows // GROUP)
    cut = (rows + GROUP) * 5 // 13 // 16 * 16
    has_up, has_down = z < nz - 1, z > 0
    ranges = ((0, cut), (cut, rows + GROUP - cut))
    orders = (("zyx", "zxy"), ("yzx", "xzy"))

    def item(i):
        k = jnp.where(i <= 2 * near, (i + 1) // 2, i - near)
        below = jnp.where(i <= 2 * near, i % 2, jnp.where(z > near, 1, 0))
        return jnp.where(below == 1, z - k, z + k)

    planes = [z] + [item(i) for i in range(1, nz)]

    def along_z(act):
        @pl.when(has_up)
        def _():
            act((blk + 2, feat))

        @pl.when(has_down)
        def _():
            act((blk - 2, feat))

    def place(i, dy):
        return planes[i] * 2 + (1 - y if dy else y)

    loads = [pltpu.make_async_copy(ref, own_in.at[t], in_sem.at[t])
             for t, ref in enumerate((img_ref, txt_ref))]
    for load in loads:
        load.start()

    barrier = pltpu.get_barrier_semaphore()

    def greet(to):
        pl.semaphore_signal(barrier, inc=1, device_id=to, device_id_type=MESH)

    for to in ((blk_y, feat), (blk, feat_x), (blk, feat_c)):
        greet(to)
    along_z(greet)

    for t in (0, 1):
        loads[t].wait()
        buf[t, blk, feat, 0:rows, :] = own_in[t, :, 0:wide]
        last = own_in[t, :, wide:wide + rem]
        for q in range(groups):
            n = min(GROUP, rows - q * GROUP)
            buf[t, blk, feat, rows:rows + n, q * rem:(q + 1) * rem] = last[q * GROUP:q * GROUP + n]

    pl.semaphore_wait(barrier, 3 + jnp.where(has_up, 1, 0) + jnp.where(has_down, 1, 0))

    sent = []

    def copy(h, t, b, f, to, sid):
        slot = buf.at[t, b, f, pl.ds(*ranges[h])]
        return pltpu.make_async_remote_copy(
            src_ref=slot, dst_ref=slot, send_sem=ssem.at[sid], recv_sem=rsem.at[h, t, b, f],
            device_id=to, device_id_type=MESH,
        )

    def send(h, t, b, f, to, cond=None):
        sid = len(sent)
        sent.append((h, t, b, f, to, cond))
        if cond is None:
            copy(h, t, b, f, to, sid).start()
        else:
            @pl.when(cond)
            def _():
                copy(h, t, b, f, to, sid).start()

    def wait_sent():
        for sid, (h, t, b, f, to, cond) in enumerate(sent):
            if cond is None:
                copy(h, t, b, f, to, sid).wait_send()
            else:
                @pl.when(cond)
                def _():
                    copy(h, t, b, f, to, sid).wait_send()

    def arrive(h, t, b, f):
        copy(h, t, b, f, (blk, feat_c), 0).wait_recv()

    def relay(h, t, i, dy, dx):
        order = orders[h][t]
        far = {"z": i, "y": dy, "x": dx}
        came = max([n for n, axis in enumerate(order) if far[axis]], default=-1)
        b, f = place(i, dy), feat_x if dx else feat
        if came >= 0:
            arrive(h, t, b, f)
        if i and order[came] == "z":
            send(h, t, b, f, (blk + 2, feat), jnp.logical_and(planes[i] < z, has_up))
            send(h, t, b, f, (blk - 2, feat), jnp.logical_and(planes[i] > z, has_down))
        for axis in order[came + 1:]:
            if axis == "z":
                send(h, t, b, f, (blk + 2, feat), has_up)
                send(h, t, b, f, (blk - 2, feat), has_down)
            else:
                send(h, t, b, f, (blk, feat_x) if axis == "x" else (blk_y, feat))
        send(h, t, b, f, (blk, feat_c), None if i == 0 and dy == 0 else c == t)

    scale, bias = scale_ref[0], bias_ref[0]

    def unpack(out, t, b):
        for q in range(groups):
            n = min(GROUP, rows - q * GROUP)
            for f in range(4):
                out[q * GROUP:q * GROUP + n, f * rem:(f + 1) * rem] = (
                    buf[t, b, f, rows:rows + n, q * rem:(q + 1) * rem])

    def hand(b):
        return pltpu.make_async_remote_copy(
            src_ref=slope_buf.at[c, b], dst_ref=slope_buf.at[c, b],
            send_sem=slope_ssem.at[b], recv_sem=slope_rsem.at[b],
            device_id=(blk, feat_c), device_id_type=MESH,
        )

    def finish(i, dy):
        b = place(i, dy)
        for h in (0, 1):
            for f in (feat_c, feat_xc):
                arrive(h, u, b, f)
                if i == 0 and dy == 0:
                    arrive(h, c, b, f)
        if i == 0 and dy == 0:
            unpack(mine, c, b)
        unpack(theirs, u, b)
        dots = dot_nt(mine[...], theirs[...])
        for f in range(4):
            dots += dot_nt(buf[c, blk, f, 0:rows, :], buf[u, b, f, 0:rows, :])
        logit = scale * dots + bias
        if i == 0 and dy == 0:
            diag = (lax.broadcasted_iota(jnp.int32, logit.shape, 0)
                    == lax.broadcasted_iota(jnp.int32, logit.shape, 1))
            value = jax.nn.sigmoid(jnp.where(diag, -logit, logit))
            value = jnp.where(diag, -value, value)
        else:
            value = jax.nn.sigmoid(logit)
        slope_buf[c, b] = value.astype(BF16)
        hand(b).start()

    def apply(i, dy):
        b = place(i, dy)
        for t in (0, 1):
            for q in range(groups):
                n = min(GROUP, rows - q * GROUP)
                own_rem[t, q * GROUP:q * GROUP + n, :] = (
                    buf[t, b, feat, rows:rows + n, q * rem:(q + 1) * rem])
        pltpu.make_async_remote_copy(
            src_ref=slope_buf.at[u, b], dst_ref=slope_buf.at[u, b],
            send_sem=slope_ssem.at[b], recv_sem=slope_rsem.at[b],
            device_id=(blk, feat_c), device_id_type=MESH,
        ).wait_recv()
        for t in (0, 1):
            slope = slope_buf[t, b]
            acc[t] += jnp.dot(slope, buf[1 - t, b, feat, 0:rows, :], preferred_element_type=F32)
            accr[t] += jnp.dot(slope, own_rem[1 - t], preferred_element_type=F32)

    acc[...] = jnp.zeros_like(acc)
    accr[...] = jnp.zeros_like(accr)

    def steps(codes):
        sent.clear()
        slopes = 0
        for step in codes:
            kind, part, i, dy, dx = step // 64, step // 16 % 4, step // 4 % 4, step // 2 % 2, step % 2
            if kind == 0:
                relay(part // 2, part % 2, i, dy, dx)
            elif kind == 1:
                finish(i, dy)
                slopes += 1
                if slopes == 2 * nz:
                    wait_sent()
            else:
                apply(i, dy)

    for inner, codes in enumerate(STEPS):
        @pl.when((near > 0) == bool(inner))
        def _():
            steps(codes)

    for t, ref in ((0, gi_ref), (1, gt_ref)):
        ref[:, 0:wide] = acc[t]
        ref[:, wide:wide + rem] = accr[t]
    for b in range(nz * 2):
        hand(b).wait_send()


def gathered(blocks, image, text, scale, bias):
    rows, width = image.shape
    wide = width // 128 * 128
    rem = width - wide
    nz = blocks // 2
    out = jax.ShapeDtypeStruct((rows, width), F32)
    image_sum, text_sum = pl.pallas_call(
        functools.partial(kernel, nz, rows, wide, rem),
        out_shape=(out, out),
        in_specs=[pl.BlockSpec(memory_space=pl.ANY)] * 2
        + [pl.BlockSpec(memory_space=pltpu.SMEM)] * 2,
        out_specs=(pl.BlockSpec(memory_space=pltpu.VMEM),) * 2,
        scratch_shapes=[
            pltpu.VMEM((2, rows, width), BF16),
            pltpu.SemaphoreType.DMA((2,)),
            pltpu.VMEM((2, blocks, 4, rows + GROUP, wide), BF16),
            pltpu.VMEM((2, blocks, rows, rows), BF16),
            pltpu.VMEM((rows, 4 * rem), BF16),
            pltpu.VMEM((rows, 4 * rem), BF16),
            pltpu.VMEM((2, rows, rem), BF16),
            pltpu.VMEM((2, rows, wide), F32),
            pltpu.VMEM((2, rows, rem), F32),
            pltpu.SemaphoreType.DMA((44 * nz,)),
            pltpu.SemaphoreType.DMA((2, 2, blocks, 4)),
            pltpu.SemaphoreType.DMA((blocks,)),
            pltpu.SemaphoreType.DMA((blocks,)),
        ],
        compiler_params=pltpu.CompilerParams(
            collective_id=0, has_side_effects=True, vmem_limit_bytes=60 * 2**20
        ),
    )(image, text, scale.reshape(1), bias.reshape(1))
    return scale * image_sum, scale * text_sum


def solution(mesh):
    in_specs = (P("blk", "feat"), P("blk", "feat"), P(), P())
    out_specs = (P("blk", "feat"), P("blk", "feat"))
    blocks, feats = mesh.shape["blk"], mesh.shape["feat"]

    def body(image, text, scale, bias):
        whole = 2 * blocks * feats * image.size * 2
        if feats == 4 and blocks == 2 * PLANES and whole <= 16 * 2**20:
            return gathered(blocks, image, text, scale, bias)
        return shards(image, text, scale, bias)

    return jax.shard_map(body, mesh=mesh, in_specs=in_specs, out_specs=out_specs, check_vma=False)
```
